256 devices in a mesh: row: 32 (over x, y, core), col: 8 (over z).
Axes of the slice: x: 4, y: 4, z: 8, core: 2. Of those that a mesh axis runs over, the one named last changes fastest.
Arguments:
- hidden_in: bfloat16 [1152, 2048], P('col', 'row'), may hold values from -21 to 21
- state: float32 [128, 2048, 1152], P('col', 'row'), may hold values from -4 to 4
- attn_norm_gain: bfloat16 [2048], replicated, may hold values from 0.099609375 to 1.8984375
- w_query: bfloat16 [2048, 2048], P(None, 'row'), may hold values from -0.125 to 0.125
- w_key: bfloat16 [2048, 2048], P(None, 'row'), may hold values from -0.125 to 0.125
- w_value: bfloat16 [2048, 2048], P(None, 'row'), may hold values from -0.125 to 0.125
- w_gate: bfloat16 [2048, 2048], P(None, 'row'), may hold values from -0.125 to 0.125
- w_decay: bfloat16 [2048, 16], replicated, may hold values from -0.125 to 0.125
- w_beta: bfloat16 [2048, 16], replicated, may hold values from -0.125 to 0.125
- decay_log: float32 [16], replicated, may hold values from -3 to 1.5
- decay_bias: float32 [16], replicated, may hold values from -2 to 1
- head_gain: float32 [128], replicated, may hold values from 0.1 to 1.9
- w_out: bfloat16 [2048, 2048], P('row'), may hold values from -0.125 to 0.125
- final_gain: bfloat16 [2048], P('row'), may hold values from 0.099609375 to 1.8984375
- lm_weight: bfloat16 [2048, 163840], P(None, ('row', 'col')), may hold values from -0.28726213 to 0.28726213
- token_ids: int32 [1152], replicated, may hold values from 0 to 163839
- ref_logprob: float32 [1152], replicated, may hold values from -16 to -6
Outputs:
- new_state: float32 [128, 2048, 1152], P('col', 'row')
- logprob: float32 [1152], replicated
- entropy: float32 [1152], replicated
- kl: float32 [1152], replicated
The draws below stay inside these ranges and needn't reach their ends.
All inputs are finite; a program needn't handle non-finite values.
Results may differ from the reference program's by a relative error of at most 0.0014.
The reference program's roundings to bfloat16 on the way (of `normed`, `mixed_heads` and `final`) count: a program that leaves them out, or rounds other values in their place, can miss the bound.
Values may be sent and summed in bfloat16 or wider, within the bound.
No kernel may reach another device: no remote copies, remote signals or barrier semaphores. Data moves between devices by JAX's collectives and lax.ppermute only.
A program may use at most 64 MiB of HBM per device.

```python
import jax
import jax.numpy as jnp
from jax import lax

D = 2048
HEADS = 16
DK = 128
DV = 128
VOCAB_DEV = 640
BATCH = 1152
VOCAB = 163840


def shared_sign(key):
    flips = jax.random.bernoulli(jax.random.fold_in(key, 101), 0.5, (D,))
    return jnp.where(flips, 1.0, -1.0).astype(jnp.float32)


def aligned_rows(key):
    level = jax.random.randint(jax.random.fold_in(key, 102), (BATCH,), 0, 3)
    chosen_rows = jnp.arange(BATCH, dtype=jnp.int32) % 5 == 0
    strength = 1.5 * jnp.exp2(level.astype(jnp.float32))
    return jnp.where(chosen_rows, strength, 0.0)


def draw_hidden_in(key, part):
    column_scale = 1.0 + 2.0 * jnp.arange(D, dtype=jnp.float32) / D
    strength = aligned_rows(key)
    base = jnp.clip(jax.random.normal(jax.random.fold_in(key, 3), (BATCH, D), jnp.float32), -4.0, 4.0)
    spread = base * column_scale[None, :]
    aligned = strength[:, None] * shared_sign(key)[None, :] + base
    values = jnp.where(strength[:, None] > 0.0, aligned, spread)
    return values.astype(jnp.bfloat16)


def draw_lm_weight(key, part):
    column_scale = 1.0 + 2.0 * jnp.arange(VOCAB, dtype=jnp.float32) / VOCAB
    base = jnp.clip(jax.random.normal(jax.random.fold_in(key, 6), (D, VOCAB), jnp.float32), -4.0, 4.0)
    base = base * column_scale[None, :] / jnp.sqrt(jnp.float32(D))
    chosen = jax.random.randint(jax.random.fold_in(key, 5), (4,), 0, VOCAB - 1)
    heights = (280.0 - 30.0 * jnp.arange(4, dtype=jnp.float32)) / jnp.float32(D)
    strength = jnp.zeros((VOCAB,), jnp.float32)
    strength = strength.at[chosen + 1].set(heights - 2.0 / jnp.float32(D))
    strength = strength.at[chosen].set(heights)
    values = jnp.where(strength[None, :] > 0.0, shared_sign(key)[:, None] * strength[None, :], base)
    return values.astype(jnp.bfloat16)


def plant(values, own_key, least, top_value):
    index_at = [jax.random.randint(jax.random.fold_in(own_key, axis), (), 0, length) for axis, length in enumerate(values.shape)]
    longest = values.shape.index(max(values.shape))
    next_to = index_at[:longest] + [(index_at[longest] + 1) % values.shape[longest]] + index_at[longest + 1:]
    return values.at[tuple(index_at)].set(least).at[tuple(next_to)].set(top_value)


def steps_of(key, shape, pieces, low, largest):
    factor_of, own = 1.0, jax.random.fold_in(key, 6)
    for dim, shards_of in pieces:
        draws = jnp.exp(jax.random.uniform(jax.random.fold_in(own, dim), (shards_of,), jnp.float32, low / len(pieces), largest / len(pieces)))
        factor_of = factor_of * jnp.repeat(draws, shape[dim] // shards_of).reshape([-1 if axis == dim else 1 for axis in range(len(shape))])
    return factor_of


def bell_draw(key, dims, scale, limit, cuts=(), kind=jnp.bfloat16):
    values = jax.random.normal(key, dims, jnp.float32) * scale
    if len(cuts) > 0:
        values = steps_of(key, dims, cuts, -0.22, 0.18) * values
    return jnp.clip(values, min=-limit, max=limit).astype(kind)


def setup_inputs(seed: int = 0) -> dict:
    keys = jax.random.split(jax.random.key(seed), 18)
    return {
        "hidden_in": draw_hidden_in(jax.random.fold_in(keys[17], 71), 0),
        "state": bell_draw(keys[1], (DK, HEADS * DV, BATCH), 0.5, 4.0, ((0, 8), (1, 32)), jnp.float32),
        "attn_norm_gain": jnp.clip(1.0 + 0.18 * jax.random.normal(keys[2], (D,), jnp.float32), 0.099609375, 1.8984375).astype(jnp.bfloat16),
        "w_query": bell_draw(keys[3], (D, HEADS * DK), D ** -0.5, 0.125, ((1, 32),)),
        "w_key": bell_draw(keys[4], (D, HEADS * DK), D ** -0.5, 0.125, ((1, 32),)),
        "w_value": bell_draw(keys[5], (D, HEADS * DV), D ** -0.5, 0.125, ((1, 32),)),
        "w_gate": bell_draw(keys[6], (D, HEADS * DV), D ** -0.5, 0.125, ((1, 32),)),
        "w_decay": bell_draw(keys[7], (D, HEADS), D ** -0.5, 0.125),
        "w_beta": bell_draw(keys[8], (D, HEADS), D ** -0.5, 0.125),
        "decay_log": jnp.clip(jax.random.uniform(keys[9], (HEADS,), jnp.float32, -3.0, 1.5), -3.0, 1.5),
        "decay_bias": jnp.clip(jax.random.uniform(keys[10], (HEADS,), jnp.float32, -2.0, 1.0), -2.0, 1.0),
        "head_gain": jnp.clip(1.0 + 0.18 * jax.random.normal(keys[11], (DV,), jnp.float32), 0.1, 1.9),
        "w_out": bell_draw(keys[12], (HEADS * DV, D), (HEADS * DV) ** -0.5, 0.125, ((0, 32),)),
        "final_gain": jnp.clip(1.0 + 0.18 * jax.random.normal(keys[13], (D,), jnp.float32), 0.099609375, 1.8984375).astype(jnp.bfloat16),
        "lm_weight": draw_lm_weight(jax.random.fold_in(keys[17], 71), 0),
        "token_ids": plant(jax.random.randint(keys[15], (BATCH,), 0, VOCAB), jax.random.fold_in(keys[15], 1), 0, VOCAB - 1).astype(jnp.int32),
        "ref_logprob": jnp.clip(jax.random.uniform(keys[16], (BATCH,), jnp.float32, -16.0, -6.0), -16.0, -6.0),
    }


def reference(hidden_in, state, attn_norm_gain, w_query, w_key, w_value, w_gate, w_decay, w_beta, decay_log, decay_bias, head_gain, w_out, final_gain, lm_weight, token_ids, ref_logprob):
    highest = lax.Precision.HIGHEST
    x = hidden_in.astype(jnp.float32)
    normed = (x * lax.rsqrt(lax.optimization_barrier(jnp.mean(x * x, axis=1, keepdims=True)) + 1e-06) * attn_norm_gain.astype(jnp.float32)).astype(jnp.bfloat16)
    qraw = lax.optimization_barrier(jnp.dot(normed, w_query, preferred_element_type=jnp.float32).astype(jnp.bfloat16)).astype(jnp.float32).reshape(BATCH, HEADS, DK)
    kraw = lax.optimization_barrier(jnp.dot(normed, w_key, preferred_element_type=jnp.float32).astype(jnp.bfloat16)).astype(jnp.float32).reshape(BATCH, HEADS, DK)
    query = (qraw * lax.rsqrt(lax.optimization_barrier(jnp.sum(qraw * qraw, axis=2, keepdims=True)) + 1e-06)).astype(jnp.bfloat16).astype(jnp.float32)
    key = (kraw * lax.rsqrt(lax.optimization_barrier(jnp.sum(kraw * kraw, axis=2, keepdims=True)) + 1e-06)).astype(jnp.bfloat16).astype(jnp.float32)
    value = jnp.dot(normed, w_value, preferred_element_type=jnp.float32).reshape(BATCH, HEADS, DV)
    gate = jnp.dot(normed, w_gate, preferred_element_type=jnp.float32).reshape(BATCH, HEADS, DV)
    decay_in = jnp.dot(normed, w_decay, preferred_element_type=jnp.float32)
    alpha = jnp.exp(-jnp.exp(decay_log)[None, :] * jax.nn.softplus(decay_in + decay_bias[None, :]))
    beta = jax.nn.sigmoid(jnp.dot(normed, w_beta, preferred_element_type=jnp.float32))
    alpha_t = alpha.T
    beta_t = beta.T
    tiles = state.reshape(DK, HEADS, DV, BATCH)
    recall = jnp.einsum('khvb,bhk->hvb', tiles, key, precision=highest)
    value_t = jnp.transpose(value, (1, 2, 0))
    write = beta_t[:, None, :] * (value_t - alpha_t[:, None, :] * recall)
    key_t = jnp.transpose(key, (2, 1, 0))
    updated = alpha_t[None, :, None, :] * tiles + key_t[:, :, None, :] * write[None]
    readout = jnp.einsum('khvb,bhk->hvb', updated, query, precision=highest)
    power = lax.optimization_barrier(jnp.mean(readout * readout, axis=1, keepdims=True))
    gate_t = jnp.transpose(gate, (1, 2, 0))
    mixed = readout * lax.rsqrt(power + 1e-05) * head_gain[None, :, None] * jax.nn.silu(gate_t)
    mixed_heads = jnp.transpose(mixed, (2, 0, 1)).reshape(BATCH, HEADS * DV).astype(jnp.bfloat16)
    hidden = x + jnp.dot(mixed_heads, w_out, preferred_element_type=jnp.float32)
    final = (hidden * lax.rsqrt(lax.optimization_barrier(jnp.mean(hidden * hidden, axis=1, keepdims=True)) + 1e-06) * final_gain.astype(jnp.float32)).astype(jnp.bfloat16)
    shards = VOCAB // VOCAB_DEV
    columns = jnp.arange(VOCAB_DEV, dtype=jnp.int32)

    def shard_step(index, carry):
        top, total, weighted, picked = carry
        piece = lax.dynamic_slice_in_dim(lm_weight, (index * VOCAB_DEV).astype(jnp.int32), VOCAB_DEV, 1)
        logits = jnp.dot(final, piece, preferred_element_type=jnp.float32)
        local_top = lax.optimization_barrier(jnp.max(logits, axis=1))
        new_top = jnp.maximum(top, local_top)
        shrink = jnp.exp(top - new_top)
        expo = jnp.exp(logits - new_top[:, None])
        total = total * shrink + lax.optimization_barrier(jnp.sum(expo, axis=1))
        weighted = weighted * shrink + lax.optimization_barrier(jnp.sum(expo * logits, axis=1))
        hits = columns[None, :] + (index * VOCAB_DEV).astype(jnp.int32) == token_ids[:, None]
        picked = picked + lax.optimization_barrier(jnp.sum(jnp.where(hits, logits, jnp.zeros_like(logits)), axis=1))
        return (new_top, total, weighted, picked)
    start = (jnp.full((BATCH,), -1e+30, jnp.float32), jnp.zeros((BATCH,), jnp.float32), jnp.zeros((BATCH,), jnp.float32), jnp.zeros((BATCH,), jnp.float32))
    top, total, weighted, picked = lax.fori_loop(jnp.int32(0), jnp.int32(shards), shard_step, start)
    lse = top + jnp.log(total)
    logprob = picked - lse
    entropy = lse - weighted / total
    gap = jnp.clip(ref_logprob - logprob, -20.0, 20.0)
    kl = jnp.minimum(jnp.exp(gap) - gap - 1.0, 10.0)
    new_state = updated.reshape(DK, HEADS * DV, BATCH)
    return (new_state, logprob, entropy, kl)
```

```python
import jax
import jax.numpy as jnp
from jax import lax
from jax.sharding import Mesh
from jax.sharding import PartitionSpec as P

D = 2048
HEADS = 16
DK = 128
DV = 128
X = "row_0"
Y = "row_1"
CORE = "row_2"
Z = "col"
XY = (X, Y)
ZC = (Z, CORE)
ROW = (X, Y, CORE)
ROW_COL = (X, Y, CORE, Z)


def swapped(array):
    return lax.ppermute(array, CORE, [(0, 1), (1, 0)])


def exchange(blocks, axes):
    return lax.all_to_all(blocks, axes, split_axis=0, concat_axis=0, tiled=True)


def to_all(array, axes):
    return exchange(jnp.broadcast_to(array, (lax.axis_size(axes), *array.shape)), axes)


def in_core_order(core, own, other, dim):
    first = jnp.where(core == 0, own, other)
    second = jnp.where(core == 0, other, own)
    return jnp.concatenate([first, second], axis=dim)


def merged(stats, dim):
    top_n, total_n, weighted_n, picked_n = stats
    top = jnp.max(top_n, axis=dim, keepdims=True)
    scale = jnp.exp(top_n - top)
    return (
        jnp.squeeze(top, dim),
        jnp.sum(total_n * scale, axis=dim),
        jnp.sum(weighted_n * scale, axis=dim),
        jnp.sum(picked_n, axis=dim),
    )


def per_device(
    hidden_in,
    state,
    attn_norm_gain,
    w_query,
    w_key,
    w_value,
    w_gate,
    w_decay,
    w_beta,
    decay_log,
    decay_bias,
    head_gain,
    w_out,
    final_gain,
    lm_weight,
    token_ids,
    ref_logprob,
):
    core = lax.axis_index(CORE)
    zed = lax.axis_index(Z)
    head = lax.axis_index(XY)
    n_xy = lax.axis_size(XY)
    n_z = lax.axis_size(Z)
    key_rows, half, batch = state.shape
    rows = hidden_in.shape[0] // 2
    vocab_dev = lm_weight.shape[1]

    kept = lax.dynamic_slice_in_dim(hidden_in, core * rows, rows, 0)
    given = lax.dynamic_slice_in_dim(hidden_in, (1 - core) * rows, rows, 0)
    x_block = in_core_order(core, kept, swapped(given), 1)
    pieces = to_all(x_block, XY)

    w_own = jnp.concatenate([w_query, w_key, w_value, w_gate], axis=1)
    w_other = swapped(w_own)
    out_other = swapped(w_out)
    lm_other = swapped(lm_weight)
    gain_block = in_core_order(core, final_gain, swapped(final_gain), 0).astype(jnp.float32)

    x_full = jnp.moveaxis(pieces, 0, 1).reshape(rows, D).astype(jnp.float32)
    normed = (
        x_full
        * lax.rsqrt(jnp.mean(x_full * x_full, axis=1, keepdims=True) + 1e-06)
        * attn_norm_gain.astype(jnp.float32)
    ).astype(jnp.bfloat16)

    def project(weight):
        return lax.dot_general(
            weight, normed, (((0,), (1,)), ((), ())), preferred_element_type=jnp.float32
        )

    own = project(w_own).reshape(4, half, rows)
    other = project(w_other).reshape(4, half, rows)
    qkvg = in_core_order(core, own, other, 1)
    small = project(jnp.concatenate([w_decay, w_beta], axis=1))
    decay_in = lax.dynamic_slice_in_dim(small, head, 1, 0)
    beta_in = lax.dynamic_slice_in_dim(small, HEADS + head, 1, 0)
    rate = jnp.exp(lax.dynamic_slice_in_dim(decay_log, head, 1, 0))[:, None]
    bias = lax.dynamic_slice_in_dim(decay_bias, head, 1, 0)[:, None]
    alpha = jnp.exp(-rate * jax.nn.softplus(decay_in + bias))
    beta = jax.nn.sigmoid(beta_in)

    raw = lax.optimization_barrier(qkvg[:2].astype(jnp.bfloat16)).astype(jnp.float32)
    unit = (raw * lax.rsqrt(jnp.sum(raw * raw, axis=1, keepdims=True) + 1e-06)).astype(
        jnp.bfloat16
    )
    unit_f = unit.astype(jnp.float32)
    meet = jnp.sum(unit_f[0] * unit_f[1], axis=0, keepdims=True)

    parts = jnp.moveaxis(unit.reshape(2, n_z, key_rows, rows), 1, 0)
    parts = jnp.broadcast_to(parts[:, None], (n_z, 2, 2, key_rows, rows))
    landed = exchange(parts.reshape(2 * n_z, 2, key_rows, rows), ZC)
    qk = jnp.moveaxis(landed, 0, 2).reshape(2, key_rows, batch).astype(jnp.float32)
    query_k, key_k = qk[0], qk[1]

    recall_p = jnp.sum(state * key_k[:, None, :], axis=0)
    answer_p = jnp.sum(state * query_k[:, None, :], axis=0)
    both = jnp.stack([recall_p, answer_p]).reshape(2, half, 2 * n_z, rows)
    both = exchange(jnp.moveaxis(both, 2, 0).astype(jnp.bfloat16), ZC)
    both = jnp.sum(both.reshape(n_z, 2, 2, half, rows).astype(jnp.float32), axis=0)
    both = jnp.moveaxis(both, 0, 1).reshape(2, DV, rows)
    recall, answer = both[0], both[1]
    value, gate = qkvg[2], qkvg[3]
    write = beta * (value - alpha * recall)
    readout = alpha * answer + meet * write
    power = jnp.mean(readout * readout, axis=0, keepdims=True)
    mixed = (
        readout * lax.rsqrt(power + 1e-05) * head_gain[:, None] * jax.nn.silu(gate)
    ).astype(jnp.bfloat16)

    first = jnp.where(core == 0, mixed[:half], mixed[half:])
    second = jnp.where(core == 0, mixed[half:], mixed[:half])

    def projected(m, w):
        return lax.dot_general(
            m, w, (((0,), (0,)), ((), ())), preferred_element_type=jnp.float32
        )

    branch = projected(first, w_out) + projected(second, out_other)
    branch = jnp.moveaxis(branch.reshape(rows, n_xy, 2 * final_gain.shape[0]), 1, 0)
    branch = jnp.sum(exchange(branch, XY), axis=0)
    hidden = x_block.astype(jnp.float32) + branch
    energy = jnp.sum(to_all(jnp.sum(hidden * hidden, axis=1), XY), axis=0)
    final = (
        hidden * lax.rsqrt(energy / D + 1e-06)[:, None] * gain_block[None, :]
    ).astype(jnp.bfloat16)

    tall = to_all(final, Z).reshape(n_z * rows, final.shape[1])
    wide = lax.all_gather(tall, XY, axis=1, tiled=True)

    sent = jnp.concatenate(
        [write.reshape(2, half, rows), jnp.broadcast_to(alpha, (2, 1, rows))], axis=1
    )
    sent = jnp.broadcast_to(sent, (n_z, 2, half + 1, rows)).reshape(2 * n_z, half + 1, rows)
    back = jnp.moveaxis(exchange(sent, ZC), 0, 1).reshape(half + 1, batch)
    new_state = back[half] * state + key_k[:, None, :] * back[None, :half]

    ids = lax.dynamic_index_in_dim(token_ids.reshape(n_z, 2, rows), core, 1, False).reshape(-1)

    def statistics(weight, owner):
        logits = jnp.dot(wide, weight, preferred_element_type=jnp.float32)
        start = ((head * 2 + owner) * n_z + zed) * vocab_dev
        hits = jnp.arange(vocab_dev, dtype=jnp.int32)[None, :] + start == ids[:, None]
        picked = jnp.sum(jnp.where(hits, logits, jnp.zeros_like(logits)), axis=1)
        top = jnp.max(logits, axis=1)
        expo = jnp.exp(logits - top[:, None])
        return top, jnp.sum(expo, axis=1), jnp.sum(expo * logits, axis=1), picked

    pair = [jnp.stack(s) for s in zip(statistics(lm_weight, core), statistics(lm_other, 1 - core))]
    stats = jnp.stack(merged(pair, 0))
    stats = jnp.stack(merged(jnp.moveaxis(to_all(stats, XY), 1, 0), 0))
    stats = to_all(stats, ZC).reshape(n_z, 2, 4, n_z * rows)
    top, total, weighted, picked = merged(jnp.moveaxis(stats, 2, 0), 0)
    lse = top + jnp.log(total)
    logprob = picked - lse
    entropy = lse - weighted / total

    def in_order(two):
        return jnp.moveaxis(two.reshape(2, n_z, rows), 0, 1).reshape(batch)

    logprob = in_order(logprob)
    entropy = in_order(entropy)
    gap = jnp.clip(ref_logprob - logprob, -20.0, 20.0)
    kl = jnp.minimum(jnp.exp(gap) - gap - 1.0, 10.0)
    return (new_state, logprob, entropy, kl)


def solution(mesh):
    split = Mesh(mesh.devices.reshape(4, 4, 2, mesh.shape["col"]), (X, Y, CORE, Z))
    in_specs = (
        P(Z, ROW),
        P(Z, ROW, None),
        P(),
        P(None, ROW),
        P(None, ROW),
        P(None, ROW),
        P(None, ROW),
        P(),
        P(),
        P(),
        P(),
        P(),
        P(ROW, None),
        P(ROW),
        P(None, ROW_COL),
        P(),
        P(),
    )
    out_specs = (P(Z, ROW, None), P(), P(), P())
    return jax.shard_map(
        per_device, mesh=split, in_specs=in_specs, out_specs=out_specs, check_vma=False
    )
```

```python
import jax
import jax.numpy as jnp
from jax import lax
from jax.sharding import Mesh
from jax.sharding import PartitionSpec as P

D = 2048
HEADS = 16
DK = 128
DV = 128
X = "row_0"
Y = "row_1"
CORE = "row_2"
Z = "col"
XY = (X, Y)
ZC = (Z, CORE)
ROW = (X, Y, CORE)
ROW_COL = (X, Y, CORE, Z)


def swapped(array):
    return lax.ppermute(array, CORE, [(0, 1), (1, 0)])


def exchange(blocks, axes):
    return lax.all_to_all(blocks, axes, split_axis=0, concat_axis=0, tiled=True)


def to_all(array, axes):
    return exchange(jnp.broadcast_to(array, (lax.axis_size(axes), *array.shape)), axes)


def in_core_order(core, own, other, dim):
    first = jnp.where(core == 0, own, other)
    second = jnp.where(core == 0, other, own)
    return jnp.concatenate([first, second], axis=dim)


def merged(stats, dim):
    top_n, total_n, weighted_n, picked_n = stats
    top = jnp.max(top_n, axis=dim, keepdims=True)
    scale = jnp.exp(top_n - top)
    return (
        jnp.squeeze(top, dim),
        jnp.sum(total_n * scale, axis=dim),
        jnp.sum(weighted_n * scale, axis=dim),
        jnp.sum(picked_n, axis=dim),
    )


def per_device(
    hidden_in,
    state,
    attn_norm_gain,
    w_query,
    w_key,
    w_value,
    w_gate,
    w_decay,
    w_beta,
    decay_log,
    decay_bias,
    head_gain,
    w_out,
    final_gain,
    lm_weight,
    token_ids,
    ref_logprob,
):
    core = lax.axis_index(CORE)
    zed = lax.axis_index(Z)
    head = lax.axis_index(XY)
    n_xy = lax.axis_size(XY)
    n_z = lax.axis_size(Z)
    key_rows, half, batch = state.shape
    rows = hidden_in.shape[0] // 2
    vocab_dev = lm_weight.shape[1]

    kept = lax.dynamic_slice_in_dim(hidden_in, core * rows, rows, 0)
    given = lax.dynamic_slice_in_dim(hidden_in, (1 - core) * rows, rows, 0)
    gain_row = final_gain[None, :]
    given = jnp.concatenate([given, gain_row])
    x_block = in_core_order(core, jnp.concatenate([kept, gain_row]), swapped(given), 1)
    pieces = to_all(x_block, XY)
    gain_full = pieces[:, rows].reshape(D).astype(jnp.float32)

    weights = (w_query, w_key, w_value, w_gate)
    w_own = jnp.concatenate(weights, axis=1)
    w_other = jnp.concatenate([swapped(w) for w in weights], axis=1)
    out_full = lax.all_gather(w_out, ROW, axis=0, tiled=True)
    lm_other = swapped(lm_weight)

    x_full = jnp.moveaxis(pieces[:, :rows], 0, 1).reshape(rows, D).astype(jnp.float32)
    normed = (
        x_full
        * lax.rsqrt(jnp.mean(x_full * x_full, axis=1, keepdims=True) + 1e-06)
        * attn_norm_gain.astype(jnp.float32)
    ).astype(jnp.bfloat16)

    def project(weight):
        return jnp.dot(normed, weight, preferred_element_type=jnp.float32)

    own = project(w_own).reshape(rows, 4, half)
    other = project(w_other).reshape(rows, 4, half)
    qkvg = in_core_order(core, own, other, 2)
    small = project(jnp.concatenate([w_decay, w_beta], axis=1))
    decay_in = lax.dynamic_slice_in_dim(small, head, 1, 1)
    beta_in = lax.dynamic_slice_in_dim(small, HEADS + head, 1, 1)
    rate = jnp.exp(lax.dynamic_slice_in_dim(decay_log, head, 1, 0))
    bias = lax.dynamic_slice_in_dim(decay_bias, head, 1, 0)
    alpha = jnp.exp(-rate * jax.nn.softplus(decay_in + bias))
    beta = jax.nn.sigmoid(beta_in)

    raw = lax.optimization_barrier(qkvg[:, :2].astype(jnp.bfloat16)).astype(jnp.float32)
    unit = (raw * lax.rsqrt(jnp.sum(raw * raw, axis=2, keepdims=True) + 1e-06)).astype(
        jnp.bfloat16
    )
    unit_f = unit.astype(jnp.float32)
    meet = jnp.sum(unit_f[:, 0] * unit_f[:, 1], axis=1, keepdims=True)

    parts = unit.reshape(rows, 2, n_z, key_rows).transpose(2, 1, 3, 0)
    landed = exchange(parts.reshape(n_z, 2 * key_rows, rows), Z)
    landed = in_core_order(core, landed, swapped(landed), 2)
    qk = jnp.moveaxis(landed, 0, 1).reshape(2, key_rows, batch).astype(jnp.float32)
    query_k, key_k = qk[0], qk[1]

    recall_p = jnp.sum(state * key_k[:, None, :], axis=0)
    answer_p = jnp.sum(state * query_k[:, None, :], axis=0)
    both = jnp.concatenate([recall_p, answer_p]).T.astype(jnp.bfloat16)
    both = exchange(both.reshape(n_z, 2 * rows, 2 * half), Z)
    both = jnp.sum(both.astype(jnp.float32), axis=0)
    kept = lax.dynamic_slice_in_dim(both, core * rows, rows, 0)
    given = lax.dynamic_slice_in_dim(both, (1 - core) * rows, rows, 0)
    both = in_core_order(
        core, kept.reshape(rows, 2, half), swapped(given).reshape(rows, 2, half), 2
    )
    recall, answer = both[:, 0], both[:, 1]
    value, gate = qkvg[:, 2], qkvg[:, 3]
    write = beta * (value - alpha * recall)
    readout = alpha * answer + meet * write
    power = jnp.mean(readout * readout, axis=1, keepdims=True)
    mixed = (
        readout * lax.rsqrt(power + 1e-05) * head_gain[None, :] * jax.nn.silu(gate)
    ).astype(jnp.bfloat16)

    mixed_full = jnp.moveaxis(to_all(mixed, XY), 0, 1).reshape(rows, D)
    hidden = x_full + jnp.dot(mixed_full, out_full, preferred_element_type=jnp.float32)
    energy = jnp.mean(hidden * hidden, axis=1, keepdims=True)
    final = (hidden * lax.rsqrt(energy + 1e-06) * gain_full[None, :]).astype(jnp.bfloat16)

    ids = lax.dynamic_index_in_dim(token_ids.reshape(n_z, 2, rows), core, 1, False)
    ids = lax.dynamic_slice_in_dim(jnp.concatenate([ids, ids]), zed, n_z, 0)

    def statistics(block, ids):
        found = []
        for weight, owner in ((lm_weight, core), (lm_other, 1 - core)):
            logits = jnp.dot(block, weight, preferred_element_type=jnp.float32)
            start = ((head * 2 + owner) * n_z + zed) * vocab_dev
            hits = jnp.arange(vocab_dev, dtype=jnp.int32)[None, :] + start == ids[:, None]
            picked = jnp.sum(jnp.where(hits, logits, jnp.zeros_like(logits)), axis=1)
            top = jnp.max(logits, axis=1)
            expo = jnp.exp(logits - top[:, None])
            found.append((top, jnp.sum(expo, axis=1), jnp.sum(expo * logits, axis=1), picked))
        return jnp.stack(merged([jnp.stack(s) for s in zip(*found)], 0))

    def along_z(block, step):
        return lax.ppermute(block, Z, [(k, (k + step) % n_z) for k in range(n_z)])

    by_distance = [None] * n_z
    by_distance[0] = statistics(final, ids[0])
    up = down = final
    cut = rows // 2
    for step in range(1, n_z // 2):
        up, down = along_z(up, 1), along_z(down, -1)
        two = statistics(
            jnp.concatenate([up, down]), jnp.concatenate([ids[n_z - step], ids[step]])
        )
        by_distance[n_z - step], by_distance[step] = two[:, :rows], two[:, rows:]
    up, down = along_z(up[:cut], 1), along_z(down[cut:], -1)
    by_distance[n_z // 2] = statistics(jnp.concatenate([up, down]), ids[n_z // 2])
    stats = jnp.stack(by_distance)
    stats = lax.dynamic_slice_in_dim(jnp.concatenate([stats, stats]), n_z - zed, n_z, 0)
    stats = jnp.moveaxis(stats, 1, 0).reshape(4, n_z * rows)

    sent = jnp.concatenate(
        [write.reshape(rows, 2, half), jnp.broadcast_to(alpha[:, :, None], (rows, 2, 1))],
        axis=2,
    )
    kept = lax.dynamic_index_in_dim(sent, core, 1, False)
    given = lax.dynamic_index_in_dim(sent, 1 - core, 1, False)
    back = to_all(in_core_order(core, kept, swapped(given), 0), Z).reshape(batch, half + 1).T
    new_state = back[half] * state + key_k[:, None, :] * back[None, :half]

    stats = jnp.stack(merged(jnp.moveaxis(to_all(stats, Z), 1, 0), 0))
    top, total, weighted, picked = merged(jnp.moveaxis(to_all(stats, XY), 1, 0), 0)
    lse = top + jnp.log(total)
    mine = jnp.stack([picked - lse, lse - weighted / total])
    logprob, entropy = in_core_order(core, mine[:, None], swapped(mine)[:, None], 1)

    def in_order(two):
        return jnp.moveaxis(two.reshape(2, n_z, rows), 0, 1).reshape(batch)

    logprob = in_order(logprob)
    entropy = in_order(entropy)
    gap = jnp.clip(ref_logprob - logprob, -20.0, 20.0)
    kl = jnp.minimum(jnp.exp(gap) - gap - 1.0, 10.0)
    return (new_state, logprob, entropy, kl)


def solution(mesh):
    split = Mesh(mesh.devices.reshape(4, 4, 2, mesh.shape["col"]), (X, Y, CORE, Z))
    in_specs = (
        P(Z, ROW),
        P(Z, ROW, None),
        P(),
        P(None, ROW),
        P(None, ROW),
        P(None, ROW),
        P(None, ROW),
        P(),
        P(),
        P(),
        P(),
        P(),
        P(ROW, None),
        P(ROW),
        P(None, ROW_COL),
        P(),
        P(),
    )
    out_specs = (P(Z, ROW, None), P(), P(), P())
    return jax.shard_map(
        per_device, mesh=split, in_specs=in_specs, out_specs=out_specs, check_vma=False
    )
```

```python
import jax
import jax.numpy as jnp
from jax import lax
from jax.experimental import pallas as pl
from jax.experimental.pallas import tpu as pltpu
from jax.sharding import Mesh
from jax.sharding import PartitionSpec as P

D = 2048
HEADS = 16
DK = 128
DV = 128
X = "row_0"
Y = "row_1"
CORE = "row_2"
Z = "col"
XY = (X, Y)
ZC = (Z, CORE)
ROW = (X, Y, CORE)
ROW_COL = (X, Y, CORE, Z)


def swapped(array):
    return lax.ppermute(array, CORE, [(0, 1), (1, 0)])


def exchange(blocks, axes):
    return lax.all_to_all(blocks, axes, split_axis=0, concat_axis=0, tiled=True)


def to_all(array, axes):
    return exchange(jnp.broadcast_to(array, (lax.axis_size(axes), *array.shape)), axes)


def in_core_order(core, own, other, dim):
    first = jnp.where(core == 0, own, other)
    second = jnp.where(core == 0, other, own)
    return jnp.concatenate([first, second], axis=dim)


def merged(stats, dim):
    top_n, total_n, weighted_n, picked_n = stats
    top = jnp.max(top_n, axis=dim, keepdims=True)
    scale = jnp.exp(top_n - top)
    return (
        jnp.squeeze(top, dim),
        jnp.sum(total_n * scale, axis=dim),
        jnp.sum(weighted_n * scale, axis=dim),
        jnp.sum(picked_n, axis=dim),
    )


def state_sums_kernel(landed_ref, state_ref, out_ref, qk_ref):
    pieces, both, width = landed_ref.shape
    key_rows, half, lanes = state_ref.shape
    step = pl.program_id(0)

    @pl.when(step == 0)
    def _():
        for k in range(pieces):
            qk_ref[:, k * width : (k + 1) * width] = landed_ref[k].astype(jnp.float32)

    for part in range(lanes // 128):
        at = pl.ds(pl.multiple_of(step * lanes + part * 128, 128), 128)
        chunk = qk_ref[:, at]
        answer = jnp.zeros((half, 128), jnp.float32)
        recall = jnp.zeros((half, 128), jnp.float32)
        for k in range(key_rows):
            tile = state_ref[k, :, part * 128 : (part + 1) * 128]
            answer += tile * chunk[k : k + 1]
            recall += tile * chunk[key_rows + k : key_rows + k + 1]
        pair = jnp.concatenate([recall, answer], axis=0).T
        out_ref[part * 128 : (part + 1) * 128, :] = pair.astype(jnp.bfloat16)


def state_sums(landed, state):
    key_rows, half, batch = state.shape
    lanes = 384
    return pl.pallas_call(
        state_sums_kernel,
        grid=(batch // lanes,),
        in_specs=[
            pl.BlockSpec(landed.shape, lambda i: (0, 0, 0)),
            pl.BlockSpec((key_rows, half, lanes), lambda i: (0, 0, i)),
        ],
        out_specs=pl.BlockSpec((lanes, 2 * half), lambda i: (i, 0)),
        out_shape=jax.ShapeDtypeStruct((batch, 2 * half), jnp.bfloat16),
        scratch_shapes=[pltpu.VMEM((2 * key_rows, batch), jnp.float32)],
        compiler_params=pltpu.CompilerParams(vmem_limit_bytes=24 * 1024 * 1024),
        cost_estimate=pl.CostEstimate(
            flops=4 * state.size, bytes_accessed=4 * state.size, transcendentals=0
        ),
    )(landed, state)


def per_device(
    hidden_in,
    state,
    attn_norm_gain,
    w_query,
    w_key,
    w_value,
    w_gate,
    w_decay,
    w_beta,
    decay_log,
    decay_bias,
    head_gain,
    w_out,
    final_gain,
    lm_weight,
    token_ids,
    ref_logprob,
):
    core = lax.axis_index(CORE)
    zed = lax.axis_index(Z)
    head = lax.axis_index(XY)
    n_xy = lax.axis_size(XY)
    n_z = lax.axis_size(Z)
    key_rows, half, batch = state.shape
    rows = hidden_in.shape[0] // 2
    vocab_dev = lm_weight.shape[1]

    x_chip = in_core_order(core, hidden_in, swapped(hidden_in), 1)
    gain_chip = in_core_order(core, final_gain, swapped(final_gain), 0)
    x_block = lax.dynamic_slice_in_dim(x_chip, core * rows, rows, 0)
    x_block = jnp.concatenate([x_block, gain_chip[None, :]])

    weights = (w_query, w_key, w_value, w_gate)
    w_other = [swapped(w) for w in weights]
    out_full = lax.all_gather(w_out, ROW, axis=0, tiled=True)
    lm_other = swapped(lm_weight)
    x_block, *weights = lax.optimization_barrier((x_block, *weights, w_decay, w_beta))
    pieces = to_all(x_block, XY)
    w_own = jnp.concatenate(weights[:4], axis=1)
    w_small = jnp.concatenate(weights[4:], axis=1)
    w_other = jnp.concatenate(w_other, axis=1)

    gain_full = pieces[:, rows].reshape(D).astype(jnp.float32)
    x_full = jnp.moveaxis(pieces[:, :rows], 0, 1).reshape(rows, D).astype(jnp.float32)
    normed = (
        x_full
        * lax.rsqrt(jnp.mean(x_full * x_full, axis=1, keepdims=True) + 1e-06)
        * attn_norm_gain.astype(jnp.float32)
    ).astype(jnp.bfloat16)

    def project(weight):
        return lax.dot_general(
            weight, normed, (((0,), (1,)), ((), ())), preferred_element_type=jnp.float32
        )

    own = project(w_own).reshape(4, half, rows)
    other = project(w_other).reshape(4, half, rows)
    qkvg = in_core_order(core, own, other, 1)
    raw = lax.optimization_barrier(qkvg[:2].astype(jnp.bfloat16)).astype(jnp.float32)
    unit = (raw * lax.rsqrt(jnp.sum(raw * raw, axis=1, keepdims=True) + 1e-06)).astype(
        jnp.bfloat16
    )

    unit_pair = in_core_order(core, unit, swapped(unit), 2)
    parts = jnp.moveaxis(unit_pair.reshape(2, n_z, key_rows, 2 * rows), 1, 0)
    landed = exchange(parts.reshape(n_z, 2 * key_rows, 2 * rows), Z)

    both = state_sums(landed, state)
    both = exchange(both.reshape(n_z, 2 * rows, 2 * half), Z)
    both = jnp.sum(both.astype(jnp.float32), axis=0)

    small = project(w_small)
    alpha = jnp.exp(
        -jnp.exp(decay_log)[:, None] * jax.nn.softplus(small[:HEADS] + decay_bias[:, None])
    )
    alpha = lax.dynamic_slice_in_dim(alpha, head, 1, 0)
    beta = lax.dynamic_slice_in_dim(jax.nn.sigmoid(small[HEADS:]), head, 1, 0)
    unit_f = unit.astype(jnp.float32)
    meet = jnp.sum(unit_f[0] * unit_f[1], axis=0, keepdims=True)
    value, gate = qkvg[2].T, qkvg[3].T
    columns = jnp.concatenate([alpha, beta, meet]).T
    alpha_c, beta_c, meet_c = columns[:, :1], columns[:, 1:2], columns[:, 2:]

    kept = lax.dynamic_slice_in_dim(both, core * rows, rows, 0)
    given = lax.dynamic_slice_in_dim(both, (1 - core) * rows, rows, 0)
    given = swapped(given)
    recall = in_core_order(core, kept[:, :half], given[:, :half], 1)
    answer = in_core_order(core, kept[:, half:], given[:, half:], 1)
    write = beta_c * (value - alpha_c * recall)
    readout = alpha_c * answer + meet_c * write
    power = jnp.mean(readout * readout, axis=1, keepdims=True)
    mixed = (
        readout * lax.rsqrt(power + 1e-05) * head_gain[None, :] * jax.nn.silu(gate)
    ).astype(jnp.bfloat16)

    mixed_full = jnp.moveaxis(to_all(mixed, XY), 0, 1).reshape(rows, D)
    hidden = x_full + jnp.dot(mixed_full, out_full, preferred_element_type=jnp.float32)
    energy = jnp.mean(hidden * hidden, axis=1, keepdims=True)
    final = (hidden * lax.rsqrt(energy + 1e-06) * gain_full[None, :]).astype(jnp.bfloat16)

    ids = lax.dynamic_index_in_dim(token_ids.reshape(n_z, 2, rows), core, 1, False)
    ids = lax.dynamic_slice_in_dim(jnp.concatenate([ids, ids]), zed, n_z, 0).T

    def statistics(block, ids):
        found = []
        for weight, owner in ((lm_weight, core), (lm_other, 1 - core)):
            logits = jnp.dot(block, weight, preferred_element_type=jnp.float32)
            start = ((head * 2 + owner) * n_z + zed) * vocab_dev
            hits = lax.broadcasted_iota(jnp.int32, logits.shape, 1) + start == ids
            picked = jnp.sum(jnp.where(hits, logits, jnp.zeros_like(logits)), axis=1)
            top = jnp.max(logits, axis=1)
            expo = jnp.exp(logits - top[:, None])
            found.append((top, jnp.sum(expo, axis=1), jnp.sum(expo * logits, axis=1), picked))
        return jnp.stack(merged([jnp.stack(s) for s in zip(*found)], 0))

    def along_z(block, step):
        return lax.ppermute(block, Z, [(k, (k + step) % n_z) for k in range(n_z)])

    by_distance = [None] * n_z
    by_distance[0] = statistics(final, ids[:, :1])
    up = down = (final[:, : D // 2], final[:, D // 2 :])
    for step in range(1, n_z // 2):
        pairs = [(along_z(u, 1), along_z(d, -1)) for u, d in zip(up, down)]
        up, down = zip(*pairs)
        block = jnp.concatenate([jnp.concatenate(p) for p in pairs], axis=1)
        back = n_z - step
        two = statistics(
            block, jnp.concatenate([ids[:, back : back + 1], ids[:, step : step + 1]])
        )
        by_distance[back], by_distance[step] = two[:, :rows], two[:, rows:]
    middle = n_z // 2
    block = jnp.concatenate([along_z(up[0], 1), along_z(down[1], -1)], axis=1)
    by_distance[middle] = statistics(block, ids[:, middle : middle + 1])
    stats = jnp.stack(by_distance)
    stats = lax.dynamic_slice_in_dim(jnp.concatenate([stats, stats]), n_z - zed, n_z, 0)
    stats = jnp.moveaxis(stats, 1, 0).reshape(4, n_z * rows)

    kept = lax.dynamic_slice_in_dim(write, core * half, half, 1)
    given = lax.dynamic_slice_in_dim(write, (1 - core) * half, half, 1)
    w_block = in_core_order(core, kept, swapped(given), 1)
    a_block = in_core_order(core, alpha, swapped(alpha), 0)
    lanes = 2 * half
    n_stats = 4 * n_z * rows // lanes
    tail = jnp.concatenate([stats.reshape(n_stats, lanes), jnp.pad(a_block, ((0, 0), (0, lanes - rows)))])
    tail = jnp.pad(tail, ((0, -tail.shape[0] % 8), (0, 0)))
    sent = to_all(jnp.concatenate([w_block, tail]), Z)
    stats = sent[:, rows : rows + n_stats].reshape(n_z, 4, n_z * rows)
    stats = jnp.stack(merged(jnp.moveaxis(stats, 1, 0), 0))
    shared = to_all(stats, XY)

    back = jnp.transpose(sent[:, :rows].reshape(n_z, rows, 2, half), (3, 0, 2, 1))
    back = back.reshape(half, batch)
    decay = sent[:, rows + n_stats : rows + n_stats + 2, :rows].reshape(batch)
    key_k = jnp.moveaxis(landed[:, key_rows:], 0, 1).reshape(key_rows, batch)
    new_state = decay * state + key_k.astype(jnp.float32)[:, None, :] * back[None]

    top, total, weighted, picked = merged(jnp.moveaxis(shared, 1, 0), 0)
    lse = top + jnp.log(total)
    mine = jnp.stack([picked - lse, lse - weighted / total])
    logprob, entropy = in_core_order(core, mine[:, None], swapped(mine)[:, None], 1)

    def in_order(two):
        return jnp.moveaxis(two.reshape(2, n_z, rows), 0, 1).reshape(batch)

    logprob = in_order(logprob)
    entropy = in_order(entropy)
    gap = jnp.clip(ref_logprob - logprob, -20.0, 20.0)
    kl = jnp.minimum(jnp.exp(gap) - gap - 1.0, 10.0)
    return (new_state, logprob, entropy, kl)


def solution(mesh):
    split = Mesh(mesh.devices.reshape(4, 4, 2, mesh.shape["col"]), (X, Y, CORE, Z))
    in_specs = (
        P(Z, ROW),
        P(Z, ROW, None),
        P(),
        P(None, ROW),
        P(None, ROW),
        P(None, ROW),
        P(None, ROW),
        P(),
        P(),
        P(),
        P(),
        P(),
        P(ROW, None),
        P(ROW),
        P(None, ROW_COL),
        P(),
        P(),
    )
    out_specs = (P(Z, ROW, None), P(), P(), P())
    return jax.shard_map(
        per_device, mesh=split, in_specs=in_specs, out_specs=out_specs, check_vma=False
    )
```

```python
import jax
import jax.numpy as jnp
from jax import lax
from jax.experimental import pallas as pl
from jax.experimental.pallas import tpu as pltpu
from jax.sharding import Mesh
from jax.sharding import PartitionSpec as P

D = 2048
HEADS = 16
DK = 128
DV = 128
X = "row_0"
Y = "row_1"
CORE = "row_2"
Z = "col"
XY = (X, Y)
ZC = (Z, CORE)
ROW = (X, Y, CORE)
ROW_COL = (X, Y, CORE, Z)


def swapped(array):
    return lax.ppermute(array, CORE, [(0, 1), (1, 0)])


def exchange(blocks, axes):
    return lax.all_to_all(blocks, axes, split_axis=0, concat_axis=0, tiled=True)


def to_all(array, axes):
    return exchange(jnp.broadcast_to(array, (lax.axis_size(axes), *array.shape)), axes)


def in_core_order(core, own, other, dim):
    first = jnp.where(core == 0, own, other)
    second = jnp.where(core == 0, other, own)
    return jnp.concatenate([first, second], axis=dim)


def merged(stats, dim):
    top_n, total_n, weighted_n, picked_n = stats
    top = jnp.max(top_n, axis=dim, keepdims=True)
    scale = jnp.exp(top_n - top)
    return (
        jnp.squeeze(top, dim),
        jnp.sum(total_n * scale, axis=dim),
        jnp.sum(weighted_n * scale, axis=dim),
        jnp.sum(picked_n, axis=dim),
    )


def state_sums_kernel(landed_ref, state_ref, out_ref, qk_ref):
    pieces, both, width = landed_ref.shape
    key_rows, half, lanes = state_ref.shape
    step = pl.program_id(0)

    @pl.when(step == 0)
    def _():
        for k in range(pieces):
            qk_ref[:, k * width : (k + 1) * width] = landed_ref[k].astype(jnp.float32)

    for part in range(lanes // 128):
        at = pl.ds(pl.multiple_of(step * lanes + part * 128, 128), 128)
        chunk = qk_ref[:, at]
        answer = jnp.zeros((half, 128), jnp.float32)
        recall = jnp.zeros((half, 128), jnp.float32)
        for k in range(key_rows):
            tile = state_ref[k, :, part * 128 : (part + 1) * 128]
            answer += tile * chunk[k : k + 1]
            recall += tile * chunk[key_rows + k : key_rows + k + 1]
        pair = jnp.concatenate([recall, answer], axis=0).T
        out_ref[part * 128 : (part + 1) * 128, :] = pair.astype(jnp.bfloat16)


def state_sums(landed, state):
    key_rows, half, batch = state.shape
    lanes = 384
    return pl.pallas_call(
        state_sums_kernel,
        grid=(batch // lanes,),
        in_specs=[
            pl.BlockSpec(landed.shape, lambda i: (0, 0, 0)),
            pl.BlockSpec((key_rows, half, lanes), lambda i: (0, 0, i)),
        ],
        out_specs=pl.BlockSpec((lanes, 2 * half), lambda i: (i, 0)),
        out_shape=jax.ShapeDtypeStruct((batch, 2 * half), jnp.bfloat16),
        scratch_shapes=[pltpu.VMEM((2 * key_rows, batch), jnp.float32)],
        compiler_params=pltpu.CompilerParams(vmem_limit_bytes=60 * 1024 * 1024),
        cost_estimate=pl.CostEstimate(
            flops=4 * state.size, bytes_accessed=4 * state.size, transcendentals=0
        ),
    )(landed, state)


def per_device(
    hidden_in,
    state,
    attn_norm_gain,
    w_query,
    w_key,
    w_value,
    w_gate,
    w_decay,
    w_beta,
    decay_log,
    decay_bias,
    head_gain,
    w_out,
    final_gain,
    lm_weight,
    token_ids,
    ref_logprob,
):
    core = lax.axis_index(CORE)
    zed = lax.axis_index(Z)
    head = lax.axis_index(XY)
    n_xy = lax.axis_size(XY)
    n_z = lax.axis_size(Z)
    key_rows, half, batch = state.shape
    rows = hidden_in.shape[0] // 2
    vocab_dev = lm_weight.shape[1]

    x_chip = in_core_order(core, hidden_in, swapped(hidden_in), 1)
    gain_chip = in_core_order(core, final_gain, swapped(final_gain), 0)
    x_block = lax.dynamic_slice_in_dim(x_chip, core * rows, rows, 0)
    x_block = jnp.concatenate([x_block, gain_chip[None, :]])

    out_full = lax.all_gather(w_out, ROW, axis=0, tiled=True)
    weights = (w_query, w_key, w_value, w_gate, w_decay, w_beta)
    x_block, weights, attn_norm_gain, decay_log, decay_bias, token_ids = lax.optimization_barrier(
        (x_block, weights, attn_norm_gain, decay_log, decay_bias, token_ids)
    )
    pieces = to_all(x_block, XY)
    w_own = jnp.concatenate(weights[:4], axis=1)
    w_other = jnp.concatenate([swapped(w) for w in weights[:4]], axis=1)
    w_small = jnp.concatenate(weights[4:], axis=1)

    gain_full = pieces[:, rows].reshape(D).astype(jnp.float32)
    x_full = jnp.moveaxis(pieces[:, :rows], 0, 1).reshape(rows, D).astype(jnp.float32)
    normed = (
        x_full
        * lax.rsqrt(jnp.mean(x_full * x_full, axis=1, keepdims=True) + 1e-06)
        * attn_norm_gain.astype(jnp.float32)
    ).astype(jnp.bfloat16)

    def project(weight):
        return lax.dot_general(
            weight, normed, (((0,), (1,)), ((), ())), preferred_element_type=jnp.float32
        )

    own = project(w_own).reshape(4, half, rows)
    other = project(w_other).reshape(4, half, rows)
    qkvg = in_core_order(core, own, other, 1)
    raw = lax.optimization_barrier(qkvg[:2].astype(jnp.bfloat16)).astype(jnp.float32)
    unit = (raw * lax.rsqrt(jnp.sum(raw * raw, axis=1, keepdims=True) + 1e-06)).astype(
        jnp.bfloat16
    )

    unit_pair = in_core_order(core, unit, swapped(unit), 2)
    parts = jnp.moveaxis(unit_pair.reshape(2, n_z, key_rows, 2 * rows), 1, 0)
    parts = parts.reshape(n_z, 2 * key_rows, 2 * rows)
    parts, lm_weight = lax.optimization_barrier((parts, lm_weight))
    lm_other = swapped(lm_weight)
    landed = exchange(parts, Z)

    both = state_sums(landed, state)
    both, lm_weight, lm_other = lax.optimization_barrier((both, lm_weight, lm_other))
    lm_both = jnp.concatenate([lm_weight, lm_other], axis=1)
    both = exchange(both.reshape(n_z, 2 * rows, 2 * half), Z)
    both = jnp.sum(both.astype(jnp.float32), axis=0)

    small = project(w_small)
    alpha = jnp.exp(
        -jnp.exp(decay_log)[:, None] * jax.nn.softplus(small[:HEADS] + decay_bias[:, None])
    )
    alpha = lax.dynamic_slice_in_dim(alpha, head, 1, 0)
    beta = lax.dynamic_slice_in_dim(jax.nn.sigmoid(small[HEADS:]), head, 1, 0)
    unit_f = unit.astype(jnp.float32)
    meet = jnp.sum(unit_f[0] * unit_f[1], axis=0, keepdims=True)
    value, gate = qkvg[2].T, qkvg[3].T
    columns = jnp.concatenate([alpha, beta, meet]).T
    alpha_c, beta_c, meet_c = columns[:, :1], columns[:, 1:2], columns[:, 2:]

    kept = lax.dynamic_slice_in_dim(both, core * rows, rows, 0)
    given = lax.dynamic_slice_in_dim(both, (1 - core) * rows, rows, 0)
    given = swapped(given)
    recall = in_core_order(core, kept[:, :half], given[:, :half], 1)
    answer = in_core_order(core, kept[:, half:], given[:, half:], 1)
    write = beta_c * (value - alpha_c * recall)
    readout = alpha_c * answer + meet_c * write
    power = jnp.mean(readout * readout, axis=1, keepdims=True)
    mixed = (
        readout * lax.rsqrt(power + 1e-05) * head_gain[None, :] * jax.nn.silu(gate)
    ).astype(jnp.bfloat16)

    mixed_full = jnp.moveaxis(to_all(mixed, XY), 0, 1).reshape(rows, D)
    hidden = x_full + jnp.dot(mixed_full, out_full, preferred_element_type=jnp.float32)
    energy = jnp.mean(hidden * hidden, axis=1, keepdims=True)
    final = (hidden * lax.rsqrt(energy + 1e-06) * gain_full[None, :]).astype(jnp.bfloat16)

    ids = lax.dynamic_index_in_dim(token_ids.reshape(n_z, 2, rows), core, 1, False)
    ids = lax.dynamic_slice_in_dim(jnp.concatenate([ids, ids]), zed, n_z, 0).T

    own_start = ((head * 2 + core) * n_z + zed) * vocab_dev
    other_start = ((head * 2 + 1 - core) * n_z + zed) * vocab_dev

    def statistics(block, ids):
        logits = jnp.dot(block, lm_both, preferred_element_type=jnp.float32)
        at = lax.broadcasted_iota(jnp.int32, logits.shape, 1)
        at = at + jnp.where(at < vocab_dev, own_start, other_start - vocab_dev)
        picked = jnp.sum(jnp.where(at == ids, logits, jnp.zeros_like(logits)), axis=1)
        top = jnp.max(logits, axis=1)
        expo = jnp.exp(logits - top[:, None])
        return jnp.stack([top, jnp.sum(expo, axis=1), jnp.sum(expo * logits, axis=1), picked])

    def along_z(block, step):
        return lax.ppermute(block, Z, [(k, (k + step) % n_z) for k in range(n_z)])

    by_distance = [None] * n_z
    by_distance[0] = statistics(final, ids[:, :1])
    up = down = (final[:, : D // 2], final[:, D // 2 :])
    for step in range(1, n_z // 2):
        pairs = [(along_z(u, 1), along_z(d, -1)) for u, d in zip(up, down)]
        up, down = zip(*pairs)
        block = jnp.concatenate([jnp.concatenate(p) for p in pairs], axis=1)
        back = n_z - step
        two = statistics(
            block, jnp.concatenate([ids[:, back : back + 1], ids[:, step : step + 1]])
        )
        by_distance[back], by_distance[step] = two[:, :rows], two[:, rows:]
    middle = n_z // 2
    block = jnp.concatenate([along_z(up[0], 1), along_z(down[1], -1)], axis=1)
    by_distance[middle] = statistics(block, ids[:, middle : middle + 1])
    stats = jnp.stack(by_distance)
    stats = lax.dynamic_slice_in_dim(jnp.concatenate([stats, stats]), n_z - zed, n_z, 0)
    stats = jnp.moveaxis(stats, 1, 0).reshape(4, n_z * rows)

    kept = lax.dynamic_slice_in_dim(write, core * half, half, 1)
    given = lax.dynamic_slice_in_dim(write, (1 - core) * half, half, 1)
    w_block = in_core_order(core, kept, swapped(given), 1)
    a_block = in_core_order(core, alpha, swapped(alpha), 0)
    lanes = 2 * half
    n_stats = 4 * n_z * rows // lanes
    tail = jnp.concatenate([stats.reshape(n_stats, lanes), jnp.pad(a_block, ((0, 0), (0, lanes - rows)))])
    tail = jnp.pad(tail, ((0, -tail.shape[0] % 8), (0, 0)))
    sent = to_all(jnp.concatenate([w_block, tail]), Z)
    stats = sent[:, rows : rows + n_stats].reshape(n_z, 4, n_z * rows)
    stats = jnp.stack(merged(jnp.moveaxis(stats, 1, 0), 0))
    shared = to_all(stats, XY)

    back = jnp.transpose(sent[:, :rows].reshape(n_z, rows, 2, half), (3, 0, 2, 1))
    back = back.reshape(half, batch)
    decay = sent[:, rows + n_stats : rows + n_stats + 2, :rows].reshape(batch)
    key_k = jnp.moveaxis(landed[:, key_rows:], 0, 1).reshape(key_rows, batch)
    new_state = decay * state + key_k.astype(jnp.float32)[:, None, :] * back[None]

    shared, new_state = lax.optimization_barrier((shared, new_state))
    top, total, weighted, picked = merged(jnp.moveaxis(shared, 1, 0), 0)
    lse = top + jnp.log(total)
    mine = jnp.stack([picked - lse, lse - weighted / total])
    logprob, entropy = in_core_order(core, mine[:, None], swapped(mine)[:, None], 1)

    def in_order(two):
        return jnp.moveaxis(two.reshape(2, n_z, rows), 0, 1).reshape(batch)

    logprob = in_order(logprob)
    entropy = in_order(entropy)
    gap = jnp.clip(ref_logprob - logprob, -20.0, 20.0)
    kl = jnp.minimum(jnp.exp(gap) - gap - 1.0, 10.0)
    return (new_state, logprob, entropy, kl)


def solution(mesh):
    split = Mesh(mesh.devices.reshape(4, 4, 2, mesh.shape["col"]), (X, Y, CORE, Z))
    in_specs = (
        P(Z, ROW),
        P(Z, ROW, None),
        P(),
        P(None, ROW),
        P(None, ROW),
        P(None, ROW),
        P(None, ROW),
        P(),
        P(),
        P(),
        P(),
        P(),
        P(ROW, None),
        P(ROW),
        P(None, ROW_COL),
        P(),
        P(),
    )
    out_specs = (P(Z, ROW, None), P(), P(), P())
    return jax.shard_map(
        per_device, mesh=split, in_specs=in_specs, out_specs=out_specs, check_vma=False
    )
```

```python
import jax
import jax.numpy as jnp
from jax import lax
from jax.experimental import pallas as pl
from jax.experimental.pallas import tpu as pltpu
from jax.sharding import Mesh
from jax.sharding import PartitionSpec as P

D = 2048
HEADS = 16
DK = 128
DV = 128
X = "row_0"
Y = "row_1"
CORE = "row_2"
Z = "col"
XY = (X, Y)
ZC = (Z, CORE)
ROW = (X, Y, CORE)
ROW_COL = (X, Y, CORE, Z)


def swapped(array):
    return lax.ppermute(array, CORE, [(0, 1), (1, 0)])


def exchange(blocks, axes):
    return lax.all_to_all(blocks, axes, split_axis=0, concat_axis=0, tiled=True)


def to_all(array, axes):
    return exchange(jnp.broadcast_to(array, (lax.axis_size(axes), *array.shape)), axes)


def in_core_order(core, own, other, dim):
    first = jnp.where(core == 0, own, other)
    second = jnp.where(core == 0, other, own)
    return jnp.concatenate([first, second], axis=dim)


def merged(stats, dim):
    top_n, total_n, weighted_n, picked_n = stats
    top = jnp.max(top_n, axis=dim, keepdims=True)
    scale = jnp.exp(top_n - top)
    return (
        jnp.squeeze(top, dim),
        jnp.sum(total_n * scale, axis=dim),
        jnp.sum(weighted_n * scale, axis=dim),
        jnp.sum(picked_n, axis=dim),
    )


def state_sums_kernel(landed_ref, state_ref, out_ref, qk_ref, held_ref, sems):
    pieces, both, width = landed_ref.shape
    chunks, key_rows, half, lanes = held_ref.shape
    copies = []
    for c in range(chunks):
        copies.append(
            pltpu.make_async_copy(
                state_ref.at[:, :, pl.ds(c * lanes, lanes)], held_ref.at[c], sems.at[c]
            )
        )
        copies[c].start()
    for k in range(pieces):
        qk_ref[:, k * width : (k + 1) * width] = landed_ref[k].astype(jnp.float32)
    for c in range(chunks):
        copies[c].wait()
        for at in range(0, lanes, 128):
            chunk = qk_ref[:, c * lanes + at : c * lanes + at + 128]
            answer = jnp.zeros((half, 128), jnp.float32)
            recall = jnp.zeros((half, 128), jnp.float32)
            for k in range(key_rows):
                tile = held_ref[c, k, :, at : at + 128]
                answer += tile * chunk[k : k + 1]
                recall += tile * chunk[key_rows + k : key_rows + k + 1]
            pair = jnp.concatenate([recall, answer], axis=0).T
            out_ref[c * lanes + at : c * lanes + at + 128, :] = pair.astype(jnp.bfloat16)


def state_sums(landed, state):
    key_rows, half, batch = state.shape
    chunks = 3
    return pl.pallas_call(
        state_sums_kernel,
        in_specs=[pl.BlockSpec(memory_space=pltpu.VMEM), pl.BlockSpec(memory_space=pl.ANY)],
        out_specs=pl.BlockSpec(memory_space=pltpu.VMEM),
        out_shape=jax.ShapeDtypeStruct((batch, 2 * half), jnp.bfloat16),
        scratch_shapes=[
            pltpu.VMEM((2 * key_rows, batch), jnp.float32),
            pltpu.VMEM((chunks, key_rows, half, batch // chunks), jnp.float32),
            pltpu.SemaphoreType.DMA((chunks,)),
        ],
        compiler_params=pltpu.CompilerParams(vmem_limit_bytes=60 * 1024 * 1024),
        cost_estimate=pl.CostEstimate(
            flops=4 * state.size, bytes_accessed=4 * state.size, transcendentals=0
        ),
    )(landed, state)


def per_device(
    hidden_in,
    state,
    attn_norm_gain,
    w_query,
    w_key,
    w_value,
    w_gate,
    w_decay,
    w_beta,
    decay_log,
    decay_bias,
    head_gain,
    w_out,
    final_gain,
    lm_weight,
    token_ids,
    ref_logprob,
):
    core = lax.axis_index(CORE)
    zed = lax.axis_index(Z)
    head = lax.axis_index(XY)
    n_xy = lax.axis_size(XY)
    n_z = lax.axis_size(Z)
    key_rows, half, batch = state.shape
    rows = hidden_in.shape[0] // 2
    vocab_dev = lm_weight.shape[1]

    x_chip = in_core_order(core, hidden_in, swapped(hidden_in), 1)
    gain_chip = in_core_order(core, final_gain, swapped(final_gain), 0)
    x_block = lax.dynamic_slice_in_dim(x_chip, core * rows, rows, 0)
    x_block = jnp.concatenate([x_block, gain_chip[None, :]])

    out_full = lax.all_gather(w_out, ROW, axis=0, tiled=True)
    weights = (w_query, w_key, w_value, w_gate)
    copies = jnp.broadcast_to(x_block, (lax.axis_size(XY), *x_block.shape))
    copies, weights, attn_norm_gain = lax.optimization_barrier((copies, weights, attn_norm_gain))
    pieces = exchange(copies, XY)
    w_own = jnp.concatenate(weights, axis=1)
    w_other = jnp.concatenate([swapped(w) for w in weights], axis=1)

    x_full = jnp.moveaxis(pieces[:, :rows], 0, 1).reshape(rows, D).astype(jnp.float32)
    normed = (
        x_full
        * lax.rsqrt(jnp.mean(x_full * x_full, axis=1, keepdims=True) + 1e-06)
        * attn_norm_gain.astype(jnp.float32)
    ).astype(jnp.bfloat16)

    def project(weight):
        return lax.dot_general(
            weight, normed, (((0,), (1,)), ((), ())), preferred_element_type=jnp.float32
        )

    own = project(w_own).reshape(4, half, rows)
    other = project(w_other).reshape(4, half, rows)
    qkvg = in_core_order(core, own, other, 1)
    raw = lax.optimization_barrier(qkvg[:2].astype(jnp.bfloat16)).astype(jnp.float32)
    unit = (raw * lax.rsqrt(jnp.sum(raw * raw, axis=1, keepdims=True) + 1e-06)).astype(
        jnp.bfloat16
    )

    unit_pair = in_core_order(core, unit, swapped(unit), 2)
    parts = jnp.moveaxis(unit_pair.reshape(2, n_z, key_rows, 2 * rows), 1, 0)
    parts = parts.reshape(n_z, 2 * key_rows, 2 * rows)
    parts, lm_weight = lax.optimization_barrier((parts, lm_weight))
    lm_other = swapped(lm_weight)
    landed = exchange(parts, Z)

    both = state_sums(landed, state)
    small_in = (w_decay, w_beta, decay_log, decay_bias, token_ids, pieces, head_gain)
    both, lm_weight, lm_other, small_in = lax.optimization_barrier(
        (both, lm_weight, lm_other, small_in)
    )
    w_decay, w_beta, decay_log, decay_bias, token_ids, pieces, head_gain = small_in
    lm_both = jnp.concatenate([lm_weight, lm_other], axis=1)
    gain_full = pieces[:, rows].reshape(D).astype(jnp.float32)
    both = exchange(both.reshape(n_z, 2 * rows, 2 * half), Z)
    both = jnp.sum(both.astype(jnp.float32), axis=0)

    small = project(jnp.concatenate([w_decay, w_beta], axis=1))
    alpha = jnp.exp(
        -jnp.exp(decay_log)[:, None] * jax.nn.softplus(small[:HEADS] + decay_bias[:, None])
    )
    alpha = lax.dynamic_slice_in_dim(alpha, head, 1, 0)
    beta = lax.dynamic_slice_in_dim(jax.nn.sigmoid(small[HEADS:]), head, 1, 0)
    unit_f = unit.astype(jnp.float32)
    meet = jnp.sum(unit_f[0] * unit_f[1], axis=0, keepdims=True)
    value, gate = qkvg[2].T, qkvg[3].T
    columns = jnp.concatenate([alpha, beta, meet]).T
    alpha_c, beta_c, meet_c = columns[:, :1], columns[:, 1:2], columns[:, 2:]

    kept = lax.dynamic_slice_in_dim(both, core * rows, rows, 0)
    given = lax.dynamic_slice_in_dim(both, (1 - core) * rows, rows, 0)
    given = swapped(given)
    recall = in_core_order(core, kept[:, :half], given[:, :half], 1)
    answer = in_core_order(core, kept[:, half:], given[:, half:], 1)
    write = beta_c * (value - alpha_c * recall)
    readout = alpha_c * answer + meet_c * write
    power = jnp.mean(readout * readout, axis=1, keepdims=True)
    mixed = (
        readout * lax.rsqrt(power + 1e-05) * head_gain[None, :] * jax.nn.silu(gate)
    ).astype(jnp.bfloat16)

    mixed_full = jnp.moveaxis(to_all(mixed, XY), 0, 1).reshape(rows, D)
    hidden = x_full + jnp.dot(mixed_full, out_full, preferred_element_type=jnp.float32)
    energy = jnp.mean(hidden * hidden, axis=1, keepdims=True)
    final = (hidden * lax.rsqrt(energy + 1e-06) * gain_full[None, :]).astype(jnp.bfloat16)

    ids = lax.dynamic_index_in_dim(token_ids.reshape(n_z, 2, rows), core, 1, False)
    ids = lax.dynamic_slice_in_dim(jnp.concatenate([ids, ids]), zed, n_z, 0).T

    own_start = ((head * 2 + core) * n_z + zed) * vocab_dev
    other_start = ((head * 2 + 1 - core) * n_z + zed) * vocab_dev

    def statistics(block, ids):
        logits = jnp.dot(block, lm_both, preferred_element_type=jnp.float32)
        at = lax.broadcasted_iota(jnp.int32, logits.shape, 1)
        at = at + jnp.where(at < vocab_dev, own_start, other_start - vocab_dev)
        picked = jnp.sum(jnp.where(at == ids, logits, jnp.zeros_like(logits)), axis=1)
        top = jnp.max(logits, axis=1)
        expo = jnp.exp(logits - top[:, None])
        return jnp.stack([top, jnp.sum(expo, axis=1), jnp.sum(expo * logits, axis=1), picked])

    def along_z(block, step):
        return lax.ppermute(block, Z, [(k, (k + step) % n_z) for k in range(n_z)])

    by_distance = [None] * n_z
    up = down = (final[:, : D // 2], final[:, D // 2 :])
    for step in range(1, n_z // 2):
        pairs = [(along_z(u, 1), along_z(d, -1)) for u, d in zip(up, down)]
        up, down = zip(*pairs)
        block = jnp.concatenate([jnp.concatenate(p) for p in pairs], axis=1)
        back = n_z - step
        two = statistics(
            block, jnp.concatenate([ids[:, back : back + 1], ids[:, step : step + 1]])
        )
        by_distance[back], by_distance[step] = two[:, :rows], two[:, rows:]
    middle = n_z // 2
    block = jnp.concatenate([along_z(up[0], 1), along_z(down[1], -1)], axis=1)
    two = statistics(
        jnp.concatenate([final, block]), jnp.concatenate([ids[:, :1], ids[:, middle : middle + 1]])
    )
    by_distance[0], by_distance[middle] = two[:, :rows], two[:, rows:]
    stats = jnp.stack(by_distance)
    stats = lax.dynamic_slice_in_dim(jnp.concatenate([stats, stats]), n_z - zed, n_z, 0)
    stats = jnp.moveaxis(stats, 1, 0).reshape(4, n_z * rows)

    kept = lax.dynamic_slice_in_dim(write, core * half, half, 1)
    given = lax.dynamic_slice_in_dim(write, (1 - core) * half, half, 1)
    w_block = in_core_order(core, kept, swapped(given), 1)
    a_block = in_core_order(core, alpha, swapped(alpha), 0)
    lanes = 2 * half
    n_stats = 4 * n_z * rows // lanes
    tail = jnp.concatenate([stats.reshape(n_stats, lanes), jnp.pad(a_block, ((0, 0), (0, lanes - rows)))])
    tail = jnp.pad(tail, ((0, -tail.shape[0] % 8), (0, 0)))
    sent = to_all(jnp.concatenate([w_block, tail]), Z)
    stats = sent[:, rows : rows + n_stats].reshape(n_z, 4, n_z * rows)
    stats = jnp.stack(merged(jnp.moveaxis(stats, 1, 0), 0))
    shared = to_all(stats, XY)

    back = jnp.transpose(sent[:, :rows].reshape(n_z, rows, 2, half), (3, 0, 2, 1))
    back = back.reshape(half, batch)
    decay = sent[:, rows + n_stats : rows + n_stats + 2, :rows].reshape(batch)
    key_k = jnp.moveaxis(landed[:, key_rows:], 0, 1).reshape(key_rows, batch)
    new_state = decay * state + key_k.astype(jnp.float32)[:, None, :] * back[None]

    shared, new_state = lax.optimization_barrier((shared, new_state))
    top, total, weighted, picked = merged(jnp.moveaxis(shared, 1, 0), 0)
    lse = top + jnp.log(total)
    mine = jnp.stack([picked - lse, lse - weighted / total])
    logprob, entropy = in_core_order(core, mine[:, None], swapped(mine)[:, None], 1)

    def in_order(two):
        return jnp.moveaxis(two.reshape(2, n_z, rows), 0, 1).reshape(batch)

    logprob = in_order(logprob)
    entropy = in_order(entropy)
    gap = jnp.clip(ref_logprob - logprob, -20.0, 20.0)
    kl = jnp.minimum(jnp.exp(gap) - gap - 1.0, 10.0)
    return (new_state, logprob, entropy, kl)


def solution(mesh):
    split = Mesh(mesh.devices.reshape(4, 4, 2, mesh.shape["col"]), (X, Y, CORE, Z))
    in_specs = (
        P(Z, ROW),
        P(Z, ROW, None),
        P(),
        P(None, ROW),
        P(None, ROW),
        P(None, ROW),
        P(None, ROW),
        P(),
        P(),
        P(),
        P(),
        P(),
        P(ROW, None),
        P(ROW),
        P(None, ROW_COL),
        P(),
        P(),
    )
    out_specs = (P(Z, ROW, None), P(), P(), P())
    return jax.shard_map(
        per_device, mesh=split, in_specs=in_specs, out_specs=out_specs, check_vma=False
    )
```

```python
import jax
import jax.numpy as jnp
from jax import lax
from jax.experimental import pallas as pl
from jax.experimental.pallas import tpu as pltpu
from jax.sharding import Mesh
from jax.sharding import PartitionSpec as P

D = 2048
HEADS = 16
DK = 128
DV = 128
X = "row_0"
Y = "row_1"
CORE = "row_2"
Z = "col"
XY = (X, Y)
ZC = (Z, CORE)
ROW = (X, Y, CORE)
ROW_COL = (X, Y, CORE, Z)


def swapped(array):
    return lax.ppermute(array, CORE, [(0, 1), (1, 0)])


def exchange(blocks, axes):
    return lax.all_to_all(blocks, axes, split_axis=0, concat_axis=0, tiled=True)


def to_all(array, axes):
    return exchange(jnp.broadcast_to(array, (lax.axis_size(axes), *array.shape)), axes)


def in_core_order(core, own, other, dim):
    first = jnp.where(core == 0, own, other)
    second = jnp.where(core == 0, other, own)
    return jnp.concatenate([first, second], axis=dim)


def merged(stats, dim):
    top_n, total_n, weighted_n, picked_n = stats
    top = jnp.max(top_n, axis=dim, keepdims=True)
    scale = jnp.exp(top_n - top)
    return (
        jnp.squeeze(top, dim),
        jnp.sum(total_n * scale, axis=dim),
        jnp.sum(weighted_n * scale, axis=dim),
        jnp.sum(picked_n, axis=dim),
    )


def state_sums_kernel(landed_ref, state_ref, out_ref, qk_ref, held_ref, sems):
    pieces, both, width = landed_ref.shape
    chunks, key_rows, half, lanes = held_ref.shape
    ahead = 3
    copies = [
        pltpu.make_async_copy(
            state_ref.at[:, :, pl.ds(c * lanes, lanes)], held_ref.at[c], sems.at[c]
        )
        for c in range(chunks)
    ]
    for c in range(ahead):
        copies[c].start()
    for k in range(pieces):
        qk_ref[:, k * width : (k + 1) * width] = landed_ref[k].astype(jnp.float32)
    for c in range(chunks):
        copies[c].wait()
        if c + ahead < chunks:
            copies[c + ahead].start()
        for at in range(0, lanes, 128):
            chunk = qk_ref[:, c * lanes + at : c * lanes + at + 128]
            answer = jnp.zeros((half, 128), jnp.float32)
            recall = jnp.zeros((half, 128), jnp.float32)
            for k in range(key_rows):
                tile = held_ref[c, k, :, at : at + 128]
                answer += tile * chunk[k : k + 1]
                recall += tile * chunk[key_rows + k : key_rows + k + 1]
            pair = jnp.concatenate([recall, answer], axis=0).T
            out_ref[c * lanes + at : c * lanes + at + 128, :] = pair.astype(jnp.bfloat16)


def state_sums(landed, state):
    key_rows, half, batch = state.shape
    chunks = batch // 128
    return pl.pallas_call(
        state_sums_kernel,
        in_specs=[pl.BlockSpec(memory_space=pltpu.VMEM), pl.BlockSpec(memory_space=pl.ANY)],
        out_specs=pl.BlockSpec(memory_space=pltpu.VMEM),
        out_shape=jax.ShapeDtypeStruct((batch, 2 * half), jnp.bfloat16),
        scratch_shapes=[
            pltpu.VMEM((2 * key_rows, batch), jnp.float32),
            pltpu.VMEM((chunks, key_rows, half, batch // chunks), jnp.float32),
            pltpu.SemaphoreType.DMA((chunks,)),
        ],
        compiler_params=pltpu.CompilerParams(vmem_limit_bytes=60 * 1024 * 1024),
        cost_estimate=pl.CostEstimate(
            flops=4 * state.size, bytes_accessed=4 * state.size, transcendentals=0
        ),
    )(landed, state)


def state_update_kernel(landed_ref, sent_ref, state_ref, out_ref, key_ref, write_ref, decay_ref):
    pieces, both, width = landed_ref.shape
    key_rows, half, lanes = state_ref.shape
    rows = width // 2
    at_decay = both_rows(rows, pieces)
    step = pl.program_id(0)

    @pl.when(step == 0)
    def _():
        for k in range(pieces):
            key_ref[:, k * width : (k + 1) * width] = landed_ref[k].astype(jnp.float32)
            turned = sent_ref[k, :rows, :].T
            for c in range(2):
                at = k * width + c * rows
                write_ref[:, at : at + rows] = turned[c * half : (c + 1) * half]
                decay_ref[:, at : at + rows] = sent_ref[k, at_decay + c : at_decay + c + 1, :rows]

    for at in range(0, lanes, 128):
        here = pl.ds(pl.multiple_of(step * lanes + at, 128), 128)
        write = write_ref[:, here]
        decay = decay_ref[:, here]
        key = key_ref[:, here]
        for k in range(key_rows):
            tile = state_ref[k, :, at : at + 128]
            row = key[key_rows + k : key_rows + k + 1]
            out_ref[k, :, at : at + 128] = decay * tile + row * write


def both_rows(rows, pieces):
    return rows + 4 * pieces * rows // 128


def state_update(landed, sent, state):
    key_rows, half, batch = state.shape
    lanes = 384
    block = pl.BlockSpec((key_rows, half, lanes), lambda i: (0, 0, i))
    return pl.pallas_call(
        state_update_kernel,
        grid=(batch // lanes,),
        in_specs=[
            pl.BlockSpec(landed.shape, lambda i: (0, 0, 0)),
            pl.BlockSpec(sent.shape, lambda i: (0, 0, 0)),
            block,
        ],
        out_specs=block,
        out_shape=jax.ShapeDtypeStruct(state.shape, jnp.float32),
        scratch_shapes=[
            pltpu.VMEM((2 * key_rows, batch), jnp.float32),
            pltpu.VMEM((half, batch), jnp.float32),
            pltpu.VMEM((1, batch), jnp.float32),
        ],
        compiler_params=pltpu.CompilerParams(vmem_limit_bytes=60 * 1024 * 1024),
        cost_estimate=pl.CostEstimate(
            flops=3 * state.size, bytes_accessed=8 * state.size, transcendentals=0
        ),
    )(landed, sent, state)


def per_device(
    hidden_in,
    state,
    attn_norm_gain,
    w_query,
    w_key,
    w_value,
    w_gate,
    w_decay,
    w_beta,
    decay_log,
    decay_bias,
    head_gain,
    w_out,
    final_gain,
    lm_weight,
    token_ids,
    ref_logprob,
):
    core = lax.axis_index(CORE)
    zed = lax.axis_index(Z)
    head = lax.axis_index(XY)
    n_xy = lax.axis_size(XY)
    n_z = lax.axis_size(Z)
    key_rows, half, batch = state.shape
    rows = hidden_in.shape[0] // 2
    vocab_dev = lm_weight.shape[1]

    x_chip = in_core_order(core, hidden_in, swapped(hidden_in), 1)
    gain_chip = in_core_order(core, final_gain, swapped(final_gain), 0)
    x_block = lax.dynamic_slice_in_dim(x_chip, core * rows, rows, 0)
    x_block = jnp.concatenate([x_block, gain_chip[None, :]])

    out_full = lax.all_gather(w_out, ROW, axis=0, tiled=True)
    weights = (w_query, w_key, w_value, w_gate)
    copies = jnp.broadcast_to(x_block, (lax.axis_size(XY), *x_block.shape))
    copies, weights, attn_norm_gain = lax.optimization_barrier((copies, weights, attn_norm_gain))
    pieces = exchange(copies, XY)
    w_other, weights = lax.optimization_barrier(([swapped(w) for w in weights], weights))
    w_own = jnp.concatenate(weights, axis=1)
    w_other = jnp.concatenate(w_other, axis=1)

    x_full = jnp.moveaxis(pieces[:, :rows], 0, 1).reshape(rows, D).astype(jnp.float32)
    normed = (
        x_full
        * lax.rsqrt(jnp.mean(x_full * x_full, axis=1, keepdims=True) + 1e-06)
        * attn_norm_gain.astype(jnp.float32)
    ).astype(jnp.bfloat16)

    def project(weight):
        return lax.dot_general(
            weight, normed, (((0,), (1,)), ((), ())), preferred_element_type=jnp.float32
        )

    own = project(w_own).reshape(4, half, rows)
    other = project(w_other).reshape(4, half, rows)
    qkvg = in_core_order(core, own, other, 1)
    raw = lax.optimization_barrier(qkvg[:2].astype(jnp.bfloat16)).astype(jnp.float32)
    unit = (raw * lax.rsqrt(jnp.sum(raw * raw, axis=1, keepdims=True) + 1e-06)).astype(
        jnp.bfloat16
    )

    unit_pair = in_core_order(core, unit, swapped(unit), 2)
    parts = jnp.moveaxis(unit_pair.reshape(2, n_z, key_rows, 2 * rows), 1, 0)
    parts = parts.reshape(n_z, 2 * key_rows, 2 * rows)
    parts, lm_weight = lax.optimization_barrier((parts, lm_weight))
    lm_other = swapped(lm_weight)
    landed = exchange(parts, Z)

    both = state_sums(landed, state)
    small_in = (w_decay, w_beta, decay_log, decay_bias, token_ids, pieces, head_gain)
    both, lm_weight, lm_other, small_in = lax.optimization_barrier(
        (both, lm_weight, lm_other, small_in)
    )
    w_decay, w_beta, decay_log, decay_bias, token_ids, pieces, head_gain = small_in
    lm_both = jnp.concatenate([lm_weight, lm_other], axis=1)
    gain_full = pieces[:, rows].reshape(D).astype(jnp.float32)
    both = exchange(both.reshape(n_z, 2 * rows, 2 * half), Z)
    both = jnp.sum(both.astype(jnp.float32), axis=0)

    small = project(jnp.concatenate([w_decay, w_beta], axis=1))
    alpha = jnp.exp(
        -jnp.exp(decay_log)[:, None] * jax.nn.softplus(small[:HEADS] + decay_bias[:, None])
    )
    alpha = lax.dynamic_slice_in_dim(alpha, head, 1, 0)
    beta = lax.dynamic_slice_in_dim(jax.nn.sigmoid(small[HEADS:]), head, 1, 0)
    unit_f = unit.astype(jnp.float32)
    meet = jnp.sum(unit_f[0] * unit_f[1], axis=0, keepdims=True)
    value, gate = qkvg[2].T, qkvg[3].T
    columns = jnp.concatenate([alpha, beta, meet]).T
    alpha_c, beta_c, meet_c = columns[:, :1], columns[:, 1:2], columns[:, 2:]

    kept = lax.dynamic_slice_in_dim(both, core * rows, rows, 0)
    given = lax.dynamic_slice_in_dim(both, (1 - core) * rows, rows, 0)
    given = swapped(given)
    recall = in_core_order(core, kept[:, :half], given[:, :half], 1)
    answer = in_core_order(core, kept[:, half:], given[:, half:], 1)
    write = beta_c * (value - alpha_c * recall)
    readout = alpha_c * answer + meet_c * write
    power = jnp.mean(readout * readout, axis=1, keepdims=True)
    mixed = (
        readout * lax.rsqrt(power + 1e-05) * head_gain[None, :] * jax.nn.silu(gate)
    ).astype(jnp.bfloat16)

    mixed_full = jnp.moveaxis(to_all(mixed, XY), 0, 1).reshape(rows, D)
    hidden = x_full + jnp.dot(mixed_full, out_full, preferred_element_type=jnp.float32)
    energy = jnp.mean(hidden * hidden, axis=1, keepdims=True)
    final = (hidden * lax.rsqrt(energy + 1e-06) * gain_full[None, :]).astype(jnp.bfloat16)

    ids = lax.dynamic_index_in_dim(token_ids.reshape(n_z, 2, rows), core, 1, False)
    ids = lax.dynamic_slice_in_dim(jnp.concatenate([ids, ids]), zed, n_z, 0).T

    own_start = ((head * 2 + core) * n_z + zed) * vocab_dev
    other_start = ((head * 2 + 1 - core) * n_z + zed) * vocab_dev

    def statistics(block, ids):
        logits = jnp.dot(block, lm_both, preferred_element_type=jnp.float32)
        at = lax.broadcasted_iota(jnp.int32, logits.shape, 1)
        at = at + jnp.where(at < vocab_dev, own_start, other_start - vocab_dev)
        picked = jnp.sum(jnp.where(at == ids, logits, jnp.zeros_like(logits)), axis=1)
        top = jnp.max(logits, axis=1)
        expo = jnp.exp(logits - top[:, None])
        return jnp.stack([top, jnp.sum(expo, axis=1), jnp.sum(expo * logits, axis=1), picked])

    def along_z(block, step):
        return lax.ppermute(block, Z, [(k, (k + step) % n_z) for k in range(n_z)])

    middle = n_z // 2
    by_distance = [None] * n_z
    by_distance[0] = statistics(final, ids[:, :1])
    up = down = (final[:, : D // 2], final[:, D // 2 :])
    for step in range(1, middle):
        pairs = [(along_z(u, 1), along_z(d, -1)) for u, d in zip(up, down)]
        up, down = zip(*pairs)
        block = jnp.concatenate([jnp.concatenate(p) for p in pairs], axis=1)
        back = n_z - step
        two = statistics(
            block, jnp.concatenate([ids[:, back : back + 1], ids[:, step : step + 1]])
        )
        by_distance[back], by_distance[step] = two[:, :rows], two[:, rows:]
    block = jnp.concatenate([along_z(up[0], 1), along_z(down[1], -1)], axis=1)
    by_distance[middle] = statistics(block, ids[:, middle : middle + 1])
    stats = jnp.stack(by_distance)
    stats = lax.dynamic_slice_in_dim(jnp.concatenate([stats, stats]), n_z - zed, n_z, 0)
    stats = jnp.moveaxis(stats, 1, 0).reshape(4, n_z * rows)

    kept = lax.dynamic_slice_in_dim(write, core * half, half, 1)
    given = lax.dynamic_slice_in_dim(write, (1 - core) * half, half, 1)
    w_block = in_core_order(core, kept, swapped(given), 1)
    a_block = in_core_order(core, alpha, swapped(alpha), 0)
    lanes = 2 * half
    n_stats = 4 * n_z * rows // lanes
    a_block = jnp.pad(a_block, ((0, 0), (0, lanes - rows)))
    tail = jnp.concatenate([stats.reshape(n_stats, lanes), a_block])
    tail = jnp.pad(tail, ((0, -tail.shape[0] % 8), (0, 0)))
    sent = to_all(jnp.concatenate([w_block, tail]), Z)
    stats = sent[:, rows : rows + n_stats].reshape(n_z, 4, n_z * rows)
    stats = jnp.stack(merged(jnp.moveaxis(stats, 1, 0), 0))
    copies = jnp.broadcast_to(stats, (lax.axis_size(XY), *stats.shape))
    copies, sent = lax.optimization_barrier((copies, sent))
    shared = exchange(copies, XY)

    new_state = state_update(landed, sent, state)
    shared, new_state = lax.optimization_barrier((shared, new_state))
    top, total, weighted, picked = merged(jnp.moveaxis(shared, 1, 0), 0)
    lse = top + jnp.log(total)
    mine = jnp.stack([picked - lse, lse - weighted / total])
    logprob, entropy = in_core_order(core, mine[:, None], swapped(mine)[:, None], 1)

    def in_order(two):
        return jnp.moveaxis(two.reshape(2, n_z, rows), 0, 1).reshape(batch)

    logprob = in_order(logprob)
    entropy = in_order(entropy)
    gap = jnp.clip(ref_logprob - logprob, -20.0, 20.0)
    kl = jnp.minimum(jnp.exp(gap) - gap - 1.0, 10.0)
    return (new_state, logprob, entropy, kl)


def solution(mesh):
    split = Mesh(mesh.devices.reshape(4, 4, 2, mesh.shape["col"]), (X, Y, CORE, Z))
    in_specs = (
        P(Z, ROW),
        P(Z, ROW, None),
        P(),
        P(None, ROW),
        P(None, ROW),
        P(None, ROW),
        P(None, ROW),
        P(),
        P(),
        P(),
        P(),
        P(),
        P(ROW, None),
        P(ROW),
        P(None, ROW_COL),
        P(),
        P(),
    )
    out_specs = (P(Z, ROW, None), P(), P(), P())
    return jax.shard_map(
        per_device, mesh=split, in_specs=in_specs, out_specs=out_specs, check_vma=False
    )
```

```python
import functools

import jax
import jax.numpy as jnp
from jax import lax
from jax.experimental import pallas as pl
from jax.experimental.pallas import tpu as pltpu
from jax.sharding import Mesh
from jax.sharding import PartitionSpec as P

D = 2048
HEADS = 16
DK = 128
DV = 128
X = "row_0"
Y = "row_1"
CORE = "row_2"
Z = "col"
XY = (X, Y)
ZC = (Z, CORE)
ROW = (X, Y, CORE)
ROW_COL = (X, Y, CORE, Z)


def swapped(array):
    return lax.ppermute(array, CORE, [(0, 1), (1, 0)])


def exchange(blocks, axes):
    return lax.all_to_all(blocks, axes, split_axis=0, concat_axis=0, tiled=True)


def to_all(array, axes):
    return exchange(jnp.broadcast_to(array, (lax.axis_size(axes), *array.shape)), axes)


def in_core_order(core, own, other, dim):
    first = jnp.where(core == 0, own, other)
    second = jnp.where(core == 0, other, own)
    return jnp.concatenate([first, second], axis=dim)


def merged(stats, dim):
    top_n, total_n, weighted_n, picked_n = stats
    top = jnp.max(top_n, axis=dim, keepdims=True)
    scale = jnp.exp(top_n - top)
    return (
        jnp.squeeze(top, dim),
        jnp.sum(total_n * scale, axis=dim),
        jnp.sum(weighted_n * scale, axis=dim),
        jnp.sum(picked_n, axis=dim),
    )


def state_sums_kernel(landed_ref, state_ref, out_ref, qk_ref, sums_ref):
    pieces, both, width = landed_ref.shape
    slab, half, batch = state_ref.shape
    key_rows = both // 2
    step = pl.program_id(0)

    @pl.when(step == 0)
    def _():
        for k in range(pieces):
            qk_ref[:, k * width : (k + 1) * width] = landed_ref[k].astype(jnp.float32)
        sums_ref[...] = jnp.zeros_like(sums_ref)

    def add(first):
        for at in range(0, batch, 128):
            chunk = qk_ref[:, at : at + 128]
            recall = sums_ref[:half, at : at + 128]
            answer = sums_ref[half:, at : at + 128]
            for k in range(slab):
                tile = state_ref[k, :, at : at + 128]
                answer += tile * chunk[first + k : first + k + 1]
                recall += tile * chunk[key_rows + first + k : key_rows + first + k + 1]
            sums_ref[:half, at : at + 128] = recall
            sums_ref[half:, at : at + 128] = answer

    for part in range(key_rows // slab):
        pl.when(step == part)(functools.partial(add, part * slab))

    @pl.when(step == pl.num_programs(0) - 1)
    def _():
        for at in range(0, batch, 128):
            out_ref[at : at + 128, :] = sums_ref[:, at : at + 128].T.astype(jnp.bfloat16)


def state_sums(landed, state):
    key_rows, half, batch = state.shape
    slab = 4
    return pl.pallas_call(
        state_sums_kernel,
        grid=(key_rows // slab,),
        in_specs=[
            pl.BlockSpec(landed.shape, lambda i: (0, 0, 0)),
            pl.BlockSpec((slab, half, batch), lambda i: (i, 0, 0)),
        ],
        out_specs=pl.BlockSpec((batch, 2 * half), lambda i: (0, 0)),
        out_shape=jax.ShapeDtypeStruct((batch, 2 * half), jnp.bfloat16),
        scratch_shapes=[
            pltpu.VMEM((2 * key_rows, batch), jnp.float32),
            pltpu.VMEM((2 * half, batch), jnp.float32),
        ],
        compiler_params=pltpu.CompilerParams(vmem_limit_bytes=12 * 1024 * 1024),
        cost_estimate=pl.CostEstimate(
            flops=4 * state.size, bytes_accessed=4 * state.size, transcendentals=0
        ),
    )(landed, pltpu.with_memory_space_constraint(state, pltpu.HBM))


def state_update_kernel(landed_ref, sent_ref, state_ref, out_ref, key_ref, write_ref, decay_ref):
    pieces, both, width = landed_ref.shape
    slab, half, batch = state_ref.shape
    key_rows = both // 2
    rows = width // 2
    at_decay = rows + 4 * pieces * rows // 128
    step = pl.program_id(0)

    @pl.when(step == 0)
    def _():
        for k in range(pieces):
            key_ref[:, k * width : (k + 1) * width] = landed_ref[k].astype(jnp.float32)
            turned = sent_ref[k, :rows, :].T
            for c in range(2):
                at = k * width + c * rows
                write_ref[:, at : at + rows] = turned[c * half : (c + 1) * half]
                decay_ref[:, at : at + rows] = sent_ref[k, at_decay + c : at_decay + c + 1, :rows]

    def update(first):
        for at in range(0, batch, 128):
            write = write_ref[:, at : at + 128]
            decay = decay_ref[:, at : at + 128]
            for k in range(slab):
                row = key_ref[key_rows + first + k : key_rows + first + k + 1, at : at + 128]
                out_ref[k, :, at : at + 128] = decay * state_ref[k, :, at : at + 128] + row * write

    for part in range(key_rows // slab):
        pl.when(step == part)(functools.partial(update, part * slab))


def state_update(landed, sent, state):
    key_rows, half, batch = state.shape
    slab = 4
    block = pl.BlockSpec((slab, half, batch), lambda i: (i, 0, 0))
    return pl.pallas_call(
        state_update_kernel,
        grid=(key_rows // slab,),
        in_specs=[
            pl.BlockSpec(landed.shape, lambda i: (0, 0, 0)),
            pl.BlockSpec(sent.shape, lambda i: (0, 0, 0)),
            block,
        ],
        out_specs=block,
        out_shape=jax.ShapeDtypeStruct(state.shape, jnp.float32),
        scratch_shapes=[
            pltpu.VMEM((2 * key_rows, batch), jnp.float32),
            pltpu.VMEM((half, batch), jnp.float32),
            pltpu.VMEM((1, batch), jnp.float32),
        ],
        compiler_params=pltpu.CompilerParams(vmem_limit_bytes=12 * 1024 * 1024),
        cost_estimate=pl.CostEstimate(
            flops=3 * state.size, bytes_accessed=8 * state.size, transcendentals=0
        ),
    )(landed, sent, pltpu.with_memory_space_constraint(state, pltpu.HBM))


def per_device(
    hidden_in,
    state,
    attn_norm_gain,
    w_query,
    w_key,
    w_value,
    w_gate,
    w_decay,
    w_beta,
    decay_log,
    decay_bias,
    head_gain,
    w_out,
    final_gain,
    lm_weight,
    token_ids,
    ref_logprob,
):
    core = lax.axis_index(CORE)
    zed = lax.axis_index(Z)
    head = lax.axis_index(XY)
    n_xy = lax.axis_size(XY)
    n_z = lax.axis_size(Z)
    key_rows, half, batch = state.shape
    rows = hidden_in.shape[0] // 2
    vocab_dev = lm_weight.shape[1]

    x_chip = in_core_order(core, hidden_in, swapped(hidden_in), 1)
    gain_chip = in_core_order(core, final_gain, swapped(final_gain), 0)
    x_block = lax.dynamic_slice_in_dim(x_chip, core * rows, rows, 0)
    x_block = jnp.concatenate([x_block, gain_chip[None, :]])

    out_full = lax.all_gather(w_out, ROW, axis=0, tiled=True)
    weights = (w_query, w_key, w_value, w_gate)
    copies = jnp.broadcast_to(x_block, (lax.axis_size(XY), *x_block.shape))
    copies, weights, attn_norm_gain = lax.optimization_barrier((copies, weights, attn_norm_gain))
    pieces = exchange(copies, XY)
    w_other, weights = lax.optimization_barrier(([swapped(w) for w in weights], weights))
    w_own = jnp.concatenate(weights, axis=1)
    w_other = jnp.concatenate(w_other, axis=1)

    x_full = jnp.moveaxis(pieces[:, :rows], 0, 1).reshape(rows, D).astype(jnp.float32)
    normed = (
        x_full
        * lax.rsqrt(jnp.mean(x_full * x_full, axis=1, keepdims=True) + 1e-06)
        * attn_norm_gain.astype(jnp.float32)
    ).astype(jnp.bfloat16)

    def project(weight):
        return lax.dot_general(
            weight, normed, (((0,), (1,)), ((), ())), preferred_element_type=jnp.float32
        )

    own = project(w_own).reshape(4, half, rows)
    other = project(w_other).reshape(4, half, rows)
    qkvg = in_core_order(core, own, other, 1)
    raw = lax.optimization_barrier(qkvg[:2].astype(jnp.bfloat16)).astype(jnp.float32)
    unit = (raw * lax.rsqrt(jnp.sum(raw * raw, axis=1, keepdims=True) + 1e-06)).astype(
        jnp.bfloat16
    )

    unit_pair = in_core_order(core, unit, swapped(unit), 2)
    parts = jnp.moveaxis(unit_pair.reshape(2, n_z, key_rows, 2 * rows), 1, 0)
    parts = parts.reshape(n_z, 2 * key_rows, 2 * rows)
    parts, lm_weight = lax.optimization_barrier((parts, lm_weight))
    lm_other = swapped(lm_weight)
    landed = exchange(parts, Z)

    both = state_sums(landed, state)
    small_in = (w_decay, w_beta, decay_log, decay_bias, token_ids, pieces, head_gain)
    both, lm_weight, lm_other, small_in = lax.optimization_barrier(
        (both, lm_weight, lm_other, small_in)
    )
    w_decay, w_beta, decay_log, decay_bias, token_ids, pieces, head_gain = small_in
    lm_both = jnp.concatenate([lm_weight, lm_other], axis=1)
    gain_full = pieces[:, rows].reshape(D).astype(jnp.float32)
    both = exchange(both.reshape(n_z, 2 * rows, 2 * half), Z)
    both = jnp.sum(both.astype(jnp.float32), axis=0)

    small = project(jnp.concatenate([w_decay, w_beta], axis=1))
    alpha = jnp.exp(
        -jnp.exp(decay_log)[:, None] * jax.nn.softplus(small[:HEADS] + decay_bias[:, None])
    )
    alpha = lax.dynamic_slice_in_dim(alpha, head, 1, 0)
    beta = lax.dynamic_slice_in_dim(jax.nn.sigmoid(small[HEADS:]), head, 1, 0)
    unit_f = unit.astype(jnp.float32)
    meet = jnp.sum(unit_f[0] * unit_f[1], axis=0, keepdims=True)
    value, gate = qkvg[2].T, qkvg[3].T
    columns = jnp.concatenate([alpha, beta, meet]).T
    alpha_c, beta_c, meet_c = columns[:, :1], columns[:, 1:2], columns[:, 2:]

    kept = lax.dynamic_slice_in_dim(both, core * rows, rows, 0)
    given = lax.dynamic_slice_in_dim(both, (1 - core) * rows, rows, 0)
    given = swapped(given)
    recall = in_core_order(core, kept[:, :half], given[:, :half], 1)
    answer = in_core_order(core, kept[:, half:], given[:, half:], 1)
    write = beta_c * (value - alpha_c * recall)
    readout = alpha_c * answer + meet_c * write
    power = jnp.mean(readout * readout, axis=1, keepdims=True)
    mixed = (
        readout * lax.rsqrt(power + 1e-05) * head_gain[None, :] * jax.nn.silu(gate)
    ).astype(jnp.bfloat16)

    mixed_full = jnp.moveaxis(to_all(mixed, XY), 0, 1).reshape(rows, D)
    hidden = x_full + jnp.dot(mixed_full, out_full, preferred_element_type=jnp.float32)
    energy = jnp.mean(hidden * hidden, axis=1, keepdims=True)
    final = (hidden * lax.rsqrt(energy + 1e-06) * gain_full[None, :]).astype(jnp.bfloat16)

    ids = lax.dynamic_index_in_dim(token_ids.reshape(n_z, 2, rows), core, 1, False)
    ids = lax.dynamic_slice_in_dim(jnp.concatenate([ids, ids]), zed, n_z, 0).T

    own_start = ((head * 2 + core) * n_z + zed) * vocab_dev
    other_start = ((head * 2 + 1 - core) * n_z + zed) * vocab_dev

    def statistics(block, ids):
        logits = jnp.dot(block, lm_both, preferred_element_type=jnp.float32)
        at = lax.broadcasted_iota(jnp.int32, logits.shape, 1)
        at = at + jnp.where(at < vocab_dev, own_start, other_start - vocab_dev)
        picked = jnp.sum(jnp.where(at == ids, logits, jnp.zeros_like(logits)), axis=1)
        top = jnp.max(logits, axis=1)
        expo = jnp.exp(logits - top[:, None])
        return jnp.stack([top, jnp.sum(expo, axis=1), jnp.sum(expo * logits, axis=1), picked])

    def along_z(block, step):
        return lax.ppermute(block, Z, [(k, (k + step) % n_z) for k in range(n_z)])

    middle = n_z // 2
    by_distance = [None] * n_z
    up = down = (final[:, : D // 2], final[:, D // 2 :])
    for step in range(1, middle):
        pairs = [(along_z(u, 1), along_z(d, -1)) for u, d in zip(up, down)]
        up, down = zip(*pairs)
        block = jnp.concatenate([jnp.concatenate(p) for p in pairs], axis=1)
        back = n_z - step
        two = statistics(
            block, jnp.concatenate([ids[:, back : back + 1], ids[:, step : step + 1]])
        )
        by_distance[back], by_distance[step] = two[:, :rows], two[:, rows:]
    block = jnp.concatenate([along_z(up[0], 1), along_z(down[1], -1)], axis=1)
    two = statistics(
        jnp.concatenate([final, block]), jnp.concatenate([ids[:, :1], ids[:, middle : middle + 1]])
    )
    by_distance[0], by_distance[middle] = two[:, :rows], two[:, rows:]
    stats = jnp.stack(by_distance)
    stats = lax.dynamic_slice_in_dim(jnp.concatenate([stats, stats]), n_z - zed, n_z, 0)
    stats = jnp.moveaxis(stats, 1, 0).reshape(4, n_z * rows)

    kept = lax.dynamic_slice_in_dim(write, core * half, half, 1)
    given = lax.dynamic_slice_in_dim(write, (1 - core) * half, half, 1)
    w_block = in_core_order(core, kept, swapped(given), 1)
    a_block = in_core_order(core, alpha, swapped(alpha), 0)
    lanes = 2 * half
    n_stats = 4 * n_z * rows // lanes
    a_block = jnp.pad(a_block, ((0, 0), (0, lanes - rows)))
    tail = jnp.concatenate([stats.reshape(n_stats, lanes), a_block])
    tail = jnp.pad(tail, ((0, -tail.shape[0] % 8), (0, 0)))
    sent = to_all(jnp.concatenate([w_block, tail]), Z)
    stats = sent[:, rows : rows + n_stats].reshape(n_z, 4, n_z * rows)
    stats = jnp.stack(merged(jnp.moveaxis(stats, 1, 0), 0))
    copies = jnp.broadcast_to(stats, (lax.axis_size(XY), *stats.shape))
    copies, sent = lax.optimization_barrier((copies, sent))
    shared = exchange(copies, XY)

    new_state = state_update(landed, sent, state)
    shared, new_state = lax.optimization_barrier((shared, new_state))
    top, total, weighted, picked = merged(jnp.moveaxis(shared, 1, 0), 0)
    lse = top + jnp.log(total)
    mine = jnp.stack([picked - lse, lse - weighted / total])
    logprob, entropy = in_core_order(core, mine[:, None], swapped(mine)[:, None], 1)

    def in_order(two):
        return jnp.moveaxis(two.reshape(2, n_z, rows), 0, 1).reshape(batch)

    logprob = in_order(logprob)
    entropy = in_order(entropy)
    gap = jnp.clip(ref_logprob - logprob, -20.0, 20.0)
    kl = jnp.minimum(jnp.exp(gap) - gap - 1.0, 10.0)
    return (new_state, logprob, entropy, kl)


def solution(mesh):
    split = Mesh(mesh.devices.reshape(4, 4, 2, mesh.shape["col"]), (X, Y, CORE, Z))
    in_specs = (
        P(Z, ROW),
        P(Z, ROW, None),
        P(),
        P(None, ROW),
        P(None, ROW),
        P(None, ROW),
        P(None, ROW),
        P(),
        P(),
        P(),
        P(),
        P(),
        P(ROW, None),
        P(ROW),
        P(None, ROW_COL),
        P(),
        P(),
    )
    out_specs = (P(Z, ROW, None), P(), P(), P())
    return jax.shard_map(
        per_device, mesh=split, in_specs=in_specs, out_specs=out_specs, check_vma=False
    )
```

```python
import functools

import jax
import jax.numpy as jnp
from jax import lax
from jax.experimental import pallas as pl
from jax.experimental.pallas import tpu as pltpu
from jax.sharding import Mesh
from jax.sharding import PartitionSpec as P

D = 2048
HEADS = 16
DK = 128
DV = 128
X = "row_0"
Y = "row_1"
CORE = "row_2"
Z = "col"
XY = (X, Y)
ZC = (Z, CORE)
ROW = (X, Y, CORE)
ROW_COL = (X, Y, CORE, Z)


def swapped(array):
    return lax.ppermute(array, CORE, [(0, 1), (1, 0)])


def exchange(blocks, axes):
    return lax.all_to_all(blocks, axes, split_axis=0, concat_axis=0, tiled=True)


def to_all(array, axes):
    return exchange(jnp.broadcast_to(array, (lax.axis_size(axes), *array.shape)), axes)


def in_core_order(core, own, other, dim):
    first = jnp.where(core == 0, own, other)
    second = jnp.where(core == 0, other, own)
    return jnp.concatenate([first, second], axis=dim)


def merged(stats, dim):
    top_n, total_n, weighted_n, picked_n = stats
    top = jnp.max(top_n, axis=dim, keepdims=True)
    scale = jnp.exp(top_n - top)
    return (
        jnp.squeeze(top, dim),
        jnp.sum(total_n * scale, axis=dim),
        jnp.sum(weighted_n * scale, axis=dim),
        jnp.sum(picked_n, axis=dim),
    )


def held_kernel(count, chunks, *refs):
    sources, out_ref, sems = refs[:count], refs[-2], refs[-1]
    copies = []
    at = 0
    for n, source in enumerate(sources):
        width = source.shape[-1]
        size = source.shape[0] // chunks
        for c in range(chunks):
            here = pl.ds(c * size, size)
            if count == 1:
                target = out_ref.at[here]
            else:
                target = out_ref.at[here, pl.ds(at, width)]
            copies.append(pltpu.make_async_copy(source.at[here], target, sems.at[n, c]))
            copies[-1].start()
        at += width
    for copy in copies:
        copy.wait()


def held(arrays, after):
    count, chunks = len(arrays), 4
    shape = (*arrays[0].shape[:-1], sum(a.shape[-1] for a in arrays))
    size = sum(a.size * a.dtype.itemsize for a in arrays)
    arrays = [pltpu.with_memory_space_constraint(a, pltpu.HBM) for a in arrays]
    return pl.pallas_call(
        functools.partial(held_kernel, count, chunks),
        in_specs=[pl.BlockSpec(memory_space=pl.ANY)] * (count + 1),
        out_specs=pl.BlockSpec(memory_space=pltpu.VMEM),
        out_shape=pltpu.VMEM(shape, arrays[0].dtype),
        scratch_shapes=[pltpu.SemaphoreType.DMA((count, chunks))],
        compiler_params=pltpu.CompilerParams(vmem_limit_bytes=12 * 1024 * 1024),
        cost_estimate=pl.CostEstimate(flops=0, bytes_accessed=2 * size, transcendentals=0),
    )(*arrays, after)


def state_sums_kernel(landed_ref, state_ref, out_ref, qk_ref):
    pieces, both, width = landed_ref.shape
    key_rows, half, batch = state_ref.shape
    for k in range(pieces):
        qk_ref[:, k * width : (k + 1) * width] = landed_ref[k].astype(jnp.float32)
    for at in range(0, batch, 128):
        chunk = qk_ref[:, at : at + 128]
        answer = jnp.zeros((half, 128), jnp.float32)
        recall = jnp.zeros((half, 128), jnp.float32)
        for k in range(key_rows):
            tile = state_ref[k, :, at : at + 128]
            answer += tile * chunk[k : k + 1]
            recall += tile * chunk[key_rows + k : key_rows + k + 1]
        pair = jnp.concatenate([recall, answer], axis=0).T
        out_ref[at : at + 128, :] = pair.astype(jnp.bfloat16)


def state_sums(landed, state):
    key_rows, half, batch = state.shape
    return pl.pallas_call(
        state_sums_kernel,
        in_specs=[pl.BlockSpec(memory_space=pltpu.VMEM)] * 2,
        out_specs=pl.BlockSpec(memory_space=pltpu.VMEM),
        out_shape=jax.ShapeDtypeStruct((batch, 2 * half), jnp.bfloat16),
        scratch_shapes=[pltpu.VMEM((2 * key_rows, batch), jnp.float32)],
        compiler_params=pltpu.CompilerParams(vmem_limit_bytes=12 * 1024 * 1024),
        cost_estimate=pl.CostEstimate(
            flops=4 * state.size, bytes_accessed=4 * state.size, transcendentals=0
        ),
    )(landed, state)


def state_update_kernel(landed_ref, sent_ref, state_ref, out_ref, key_ref, write_ref, decay_ref):
    pieces, both, width = landed_ref.shape
    slab, half, batch = state_ref.shape
    key_rows = both // 2
    rows = width // 2
    at_decay = rows + 4 * pieces * rows // 128
    step = pl.program_id(0)

    @pl.when(step == 0)
    def _():
        for k in range(pieces):
            key_ref[:, k * width : (k + 1) * width] = landed_ref[k].astype(jnp.float32)
            turned = sent_ref[k, :rows, :].T
            for c in range(2):
                at = k * width + c * rows
                write_ref[:, at : at + rows] = turned[c * half : (c + 1) * half]
                decay_ref[:, at : at + rows] = sent_ref[k, at_decay + c : at_decay + c + 1, :rows]

    def update(first):
        for at in range(0, batch, 128):
            write = write_ref[:, at : at + 128]
            decay = decay_ref[:, at : at + 128]
            for k in range(slab):
                row = key_ref[key_rows + first + k : key_rows + first + k + 1, at : at + 128]
                out_ref[k, :, at : at + 128] = decay * state_ref[k, :, at : at + 128] + row * write

    for part in range(key_rows // slab):
        pl.when(step == part)(functools.partial(update, part * slab))


def state_update(landed, sent, state):
    key_rows, half, batch = state.shape
    slab = 4
    block = pl.BlockSpec((slab, half, batch), lambda i: (i, 0, 0))
    return pl.pallas_call(
        state_update_kernel,
        grid=(key_rows // slab,),
        in_specs=[
            pl.BlockSpec(landed.shape, lambda i: (0, 0, 0)),
            pl.BlockSpec(sent.shape, lambda i: (0, 0, 0)),
            block,
        ],
        out_specs=block,
        out_shape=jax.ShapeDtypeStruct(state.shape, jnp.float32),
        scratch_shapes=[
            pltpu.VMEM((2 * key_rows, batch), jnp.float32),
            pltpu.VMEM((half, batch), jnp.float32),
            pltpu.VMEM((1, batch), jnp.float32),
        ],
        compiler_params=pltpu.CompilerParams(vmem_limit_bytes=12 * 1024 * 1024),
        cost_estimate=pl.CostEstimate(
            flops=3 * state.size, bytes_accessed=8 * state.size, transcendentals=0
        ),
    )(landed, sent, pltpu.with_memory_space_constraint(state, pltpu.HBM))


def per_device(
    hidden_in,
    state,
    attn_norm_gain,
    w_query,
    w_key,
    w_value,
    w_gate,
    w_decay,
    w_beta,
    decay_log,
    decay_bias,
    head_gain,
    w_out,
    final_gain,
    lm_weight,
    token_ids,
    ref_logprob,
):
    core = lax.axis_index(CORE)
    zed = lax.axis_index(Z)
    head = lax.axis_index(XY)
    n_xy = lax.axis_size(XY)
    n_z = lax.axis_size(Z)
    key_rows, half, batch = state.shape
    rows = hidden_in.shape[0] // 2
    vocab_dev = lm_weight.shape[1]

    x_chip = in_core_order(core, hidden_in, swapped(hidden_in), 1)
    gain_chip = in_core_order(core, final_gain, swapped(final_gain), 0)
    x_block = lax.dynamic_slice_in_dim(x_chip, core * rows, rows, 0)
    x_block = jnp.concatenate([x_block, gain_chip[None, :]])

    out_full = lax.all_gather(w_out, ROW, axis=0, tiled=True)
    weights = (w_query, w_key, w_value, w_gate)
    copies = jnp.broadcast_to(x_block, (lax.axis_size(XY), *x_block.shape))
    copies, weights, attn_norm_gain = lax.optimization_barrier((copies, weights, attn_norm_gain))
    pieces = exchange(copies, XY)
    w_other, weights = lax.optimization_barrier(([swapped(w) for w in weights], weights))
    w_own = jnp.concatenate(weights, axis=1)
    w_other = jnp.concatenate(w_other, axis=1)

    x_full = jnp.moveaxis(pieces[:, :rows], 0, 1).reshape(rows, D).astype(jnp.float32)
    normed = (
        x_full
        * lax.rsqrt(jnp.mean(x_full * x_full, axis=1, keepdims=True) + 1e-06)
        * attn_norm_gain.astype(jnp.float32)
    ).astype(jnp.bfloat16)

    def project(weight):
        return lax.dot_general(
            weight, normed, (((0,), (1,)), ((), ())), preferred_element_type=jnp.float32
        )

    own = project(w_own).reshape(4, half, rows)
    other = project(w_other).reshape(4, half, rows)
    qkvg = in_core_order(core, own, other, 1)
    raw = lax.optimization_barrier(qkvg[:2].astype(jnp.bfloat16)).astype(jnp.float32)
    unit = (raw * lax.rsqrt(jnp.sum(raw * raw, axis=1, keepdims=True) + 1e-06)).astype(
        jnp.bfloat16
    )

    unit_pair = in_core_order(core, unit, swapped(unit), 2)
    parts = jnp.moveaxis(unit_pair.reshape(2, n_z, key_rows, 2 * rows), 1, 0)
    parts = parts.reshape(n_z, 2 * key_rows, 2 * rows)
    parts, lm_weight, after = lax.optimization_barrier((parts, lm_weight, head_gain))
    state_held = held([state], after)
    lm_other = swapped(lm_weight)
    landed = exchange(parts, Z)

    both = state_sums(landed, state_held)
    small_in = (w_decay, w_beta, decay_log, decay_bias, token_ids, pieces, head_gain)
    both, lm_weight, lm_other, small_in = lax.optimization_barrier(
        (both, lm_weight, lm_other, small_in)
    )
    w_decay, w_beta, decay_log, decay_bias, token_ids, pieces, head_gain = small_in
    lm_both = held([lm_weight, lm_other], head_gain)
    gain_full = pieces[:, rows].reshape(D).astype(jnp.float32)
    both = exchange(both.reshape(n_z, 2 * rows, 2 * half), Z)
    both = jnp.sum(both.astype(jnp.float32), axis=0)

    small = project(jnp.concatenate([w_decay, w_beta], axis=1))
    alpha = jnp.exp(
        -jnp.exp(decay_log)[:, None] * jax.nn.softplus(small[:HEADS] + decay_bias[:, None])
    )
    alpha = lax.dynamic_slice_in_dim(alpha, head, 1, 0)
    beta = lax.dynamic_slice_in_dim(jax.nn.sigmoid(small[HEADS:]), head, 1, 0)
    unit_f = unit.astype(jnp.float32)
    meet = jnp.sum(unit_f[0] * unit_f[1], axis=0, keepdims=True)
    value, gate = qkvg[2].T, qkvg[3].T
    columns = jnp.concatenate([alpha, beta, meet]).T
    alpha_c, beta_c, meet_c = columns[:, :1], columns[:, 1:2], columns[:, 2:]

    kept = lax.dynamic_slice_in_dim(both, core * rows, rows, 0)
    given = lax.dynamic_slice_in_dim(both, (1 - core) * rows, rows, 0)
    given = swapped(given)
    recall = in_core_order(core, kept[:, :half], given[:, :half], 1)
    answer = in_core_order(core, kept[:, half:], given[:, half:], 1)
    write = beta_c * (value - alpha_c * recall)
    readout = alpha_c * answer + meet_c * write
    power = jnp.mean(readout * readout, axis=1, keepdims=True)
    mixed = (
        readout * lax.rsqrt(power + 1e-05) * head_gain[None, :] * jax.nn.silu(gate)
    ).astype(jnp.bfloat16)

    copies = jnp.broadcast_to(mixed, (lax.axis_size(XY), *mixed.shape))
    copies, after = lax.optimization_barrier((copies, head_gain))
    out_held = held([out_full], after)
    mixed_full = jnp.moveaxis(exchange(copies, XY), 0, 1).reshape(rows, D)
    hidden = x_full + jnp.dot(mixed_full, out_held, preferred_element_type=jnp.float32)
    energy = jnp.mean(hidden * hidden, axis=1, keepdims=True)
    final = (hidden * lax.rsqrt(energy + 1e-06) * gain_full[None, :]).astype(jnp.bfloat16)

    ids = lax.dynamic_index_in_dim(token_ids.reshape(n_z, 2, rows), core, 1, False)
    ids = lax.dynamic_slice_in_dim(jnp.concatenate([ids, ids]), zed, n_z, 0).T

    own_start = ((head * 2 + core) * n_z + zed) * vocab_dev
    other_start = ((head * 2 + 1 - core) * n_z + zed) * vocab_dev

    def statistics(block, ids):
        logits = jnp.dot(block, lm_both, preferred_element_type=jnp.float32)
        at = lax.broadcasted_iota(jnp.int32, logits.shape, 1)
        at = at + jnp.where(at < vocab_dev, own_start, other_start - vocab_dev)
        picked = jnp.sum(jnp.where(at == ids, logits, jnp.zeros_like(logits)), axis=1)
        top = jnp.max(logits, axis=1)
        expo = jnp.exp(logits - top[:, None])
        return jnp.stack([top, jnp.sum(expo, axis=1), jnp.sum(expo * logits, axis=1), picked])

    def along_z(block, step):
        return lax.ppermute(block, Z, [(k, (k + step) % n_z) for k in range(n_z)])

    middle = n_z // 2
    by_distance = [None] * n_z
    up = down = (final[:, : D // 2], final[:, D // 2 :])
    for step in range(1, middle):
        pairs = [(along_z(u, 1), along_z(d, -1)) for u, d in zip(up, down)]
        up, down = zip(*pairs)
        block = jnp.concatenate([jnp.concatenate(p) for p in pairs], axis=1)
        back = n_z - step
        two = statistics(
            block, jnp.concatenate([ids[:, back : back + 1], ids[:, step : step + 1]])
        )
        by_distance[back], by_distance[step] = two[:, :rows], two[:, rows:]
    block = jnp.concatenate([along_z(up[0], 1), along_z(down[1], -1)], axis=1)
    two = statistics(
        jnp.concatenate([final, block]), jnp.concatenate([ids[:, :1], ids[:, middle : middle + 1]])
    )
    by_distance[0], by_distance[middle] = two[:, :rows], two[:, rows:]
    stats = jnp.stack(by_distance)
    stats = lax.dynamic_slice_in_dim(jnp.concatenate([stats, stats]), n_z - zed, n_z, 0)
    stats = jnp.moveaxis(stats, 1, 0).reshape(4, n_z * rows)

    kept = lax.dynamic_slice_in_dim(write, core * half, half, 1)
    given = lax.dynamic_slice_in_dim(write, (1 - core) * half, half, 1)
    w_block = in_core_order(core, kept, swapped(given), 1)
    a_block = in_core_order(core, alpha, swapped(alpha), 0)
    lanes = 2 * half
    n_stats = 4 * n_z * rows // lanes
    a_block = jnp.pad(a_block, ((0, 0), (0, lanes - rows)))
    tail = jnp.concatenate([stats.reshape(n_stats, lanes), a_block])
    tail = jnp.pad(tail, ((0, -tail.shape[0] % 8), (0, 0)))
    sent = to_all(jnp.concatenate([w_block, tail]), Z)
    stats = sent[:, rows : rows + n_stats].reshape(n_z, 4, n_z * rows)
    stats = jnp.stack(merged(jnp.moveaxis(stats, 1, 0), 0))
    copies = jnp.broadcast_to(stats, (lax.axis_size(XY), *stats.shape))
    copies, sent = lax.optimization_barrier((copies, sent))
    shared = exchange(copies, XY)

    new_state = state_update(landed, sent, state)
    shared, new_state = lax.optimization_barrier((shared, new_state))
    top, total, weighted, picked = merged(jnp.moveaxis(shared, 1, 0), 0)
    lse = top + jnp.log(total)
    mine = jnp.stack([picked - lse, lse - weighted / total])
    logprob, entropy = in_core_order(core, mine[:, None], swapped(mine)[:, None], 1)

    def in_order(two):
        return jnp.moveaxis(two.reshape(2, n_z, rows), 0, 1).reshape(batch)

    logprob = in_order(logprob)
    entropy = in_order(entropy)
    gap = jnp.clip(ref_logprob - logprob, -20.0, 20.0)
    kl = jnp.minimum(jnp.exp(gap) - gap - 1.0, 10.0)
    return (new_state, logprob, entropy, kl)


def solution(mesh):
    split = Mesh(mesh.devices.reshape(4, 4, 2, mesh.shape["col"]), (X, Y, CORE, Z))
    in_specs = (
        P(Z, ROW),
        P(Z, ROW, None),
        P(),
        P(None, ROW),
        P(None, ROW),
        P(None, ROW),
        P(None, ROW),
        P(),
        P(),
        P(),
        P(),
        P(),
        P(ROW, None),
        P(ROW),
        P(None, ROW_COL),
        P(),
        P(),
    )
    out_specs = (P(Z, ROW, None), P(), P(), P())
    return jax.shard_map(
        per_device, mesh=split, in_specs=in_specs, out_specs=out_specs, check_vma=False
    )
```

```python
import functools

import jax
import jax.numpy as jnp
from jax import lax
from jax.experimental import pallas as pl
from jax.experimental.pallas import tpu as pltpu
from jax.sharding import Mesh
from jax.sharding import PartitionSpec as P

D = 2048
HEADS = 16
DK = 128
DV = 128
X = "row_0"
Y = "row_1"
CORE = "row_2"
Z = "col"
XY = (X, Y)
ZC = (Z, CORE)
ROW = (X, Y, CORE)
ROW_COL = (X, Y, CORE, Z)


def swapped(array):
    return lax.ppermute(array, CORE, [(0, 1), (1, 0)])


def exchange(blocks, axes):
    return lax.all_to_all(blocks, axes, split_axis=0, concat_axis=0, tiled=True)


def to_all(array, axes):
    return exchange(jnp.broadcast_to(array, (lax.axis_size(axes), *array.shape)), axes)


def in_core_order(core, own, other, dim):
    first = jnp.where(core == 0, own, other)
    second = jnp.where(core == 0, other, own)
    return jnp.concatenate([first, second], axis=dim)


def merged(stats, dim):
    top_n, total_n, weighted_n, picked_n = stats
    top = jnp.max(top_n, axis=dim, keepdims=True)
    scale = jnp.exp(top_n - top)
    return (
        jnp.squeeze(top, dim),
        jnp.sum(total_n * scale, axis=dim),
        jnp.sum(weighted_n * scale, axis=dim),
        jnp.sum(picked_n, axis=dim),
    )


def held_kernel(count, chunks, *refs):
    sources, out_ref, sems = refs[:count], refs[-2], refs[-1]
    copies = []
    at = 0
    for n, source in enumerate(sources):
        width = source.shape[-1]
        size = source.shape[0] // chunks
        for c in range(chunks):
            here = pl.ds(c * size, size)
            if count == 1:
                target = out_ref.at[here]
            else:
                target = out_ref.at[here, pl.ds(at, width)]
            copies.append(pltpu.make_async_copy(source.at[here], target, sems.at[n, c]))
            copies[-1].start()
        at += width
    for copy in copies:
        copy.wait()


def held(arrays, after):
    count, chunks = len(arrays), 4
    shape = (*arrays[0].shape[:-1], sum(a.shape[-1] for a in arrays))
    size = sum(a.size * a.dtype.itemsize for a in arrays)
    arrays = [pltpu.with_memory_space_constraint(a, pltpu.HBM) for a in arrays]
    return pl.pallas_call(
        functools.partial(held_kernel, count, chunks),
        in_specs=[pl.BlockSpec(memory_space=pl.ANY)] * (count + 1),
        out_specs=pl.BlockSpec(memory_space=pltpu.VMEM),
        out_shape=pltpu.VMEM(shape, arrays[0].dtype),
        scratch_shapes=[pltpu.SemaphoreType.DMA((count, chunks))],
        compiler_params=pltpu.CompilerParams(vmem_limit_bytes=12 * 1024 * 1024),
        cost_estimate=pl.CostEstimate(flops=0, bytes_accessed=2 * size, transcendentals=0),
    )(*arrays, after)


def state_sums_kernel(landed_ref, state_ref, out_ref, qk_ref):
    pieces, both, width = landed_ref.shape
    key_rows, half, batch = state_ref.shape
    for k in range(pieces):
        qk_ref[:, k * width : (k + 1) * width] = landed_ref[k].astype(jnp.float32)
    for at in range(0, batch, 128):
        chunk = qk_ref[:, at : at + 128]
        answer = jnp.zeros((half, 128), jnp.float32)
        recall = jnp.zeros((half, 128), jnp.float32)
        for k in range(key_rows):
            tile = state_ref[k, :, at : at + 128]
            answer += tile * chunk[k : k + 1]
            recall += tile * chunk[key_rows + k : key_rows + k + 1]
        pair = jnp.concatenate([recall, answer], axis=0).T
        out_ref[at : at + 128, :] = pair.astype(jnp.bfloat16)


def state_sums(landed, state):
    key_rows, half, batch = state.shape
    return pl.pallas_call(
        state_sums_kernel,
        in_specs=[pl.BlockSpec(memory_space=pltpu.VMEM)] * 2,
        out_specs=pl.BlockSpec(memory_space=pltpu.VMEM),
        out_shape=jax.ShapeDtypeStruct((batch, 2 * half), jnp.bfloat16),
        scratch_shapes=[pltpu.VMEM((2 * key_rows, batch), jnp.float32)],
        compiler_params=pltpu.CompilerParams(vmem_limit_bytes=12 * 1024 * 1024),
        cost_estimate=pl.CostEstimate(
            flops=4 * state.size, bytes_accessed=4 * state.size, transcendentals=0
        ),
    )(landed, pltpu.with_memory_space_constraint(state, pltpu.VMEM))


def state_update_kernel(landed_ref, sent_ref, state_ref, out_ref, key_ref, write_ref, decay_ref):
    pieces, both, width = landed_ref.shape
    slab, half, batch = state_ref.shape
    key_rows = both // 2
    rows = width // 2
    at_decay = rows + 4 * pieces * rows // 128
    step = pl.program_id(0)

    @pl.when(step == 0)
    def _():
        for k in range(pieces):
            key_ref[:, k * width : (k + 1) * width] = landed_ref[k].astype(jnp.float32)
            turned = sent_ref[k, :rows, :].T
            for c in range(2):
                at = k * width + c * rows
                write_ref[:, at : at + rows] = turned[c * half : (c + 1) * half]
                decay_ref[:, at : at + rows] = sent_ref[k, at_decay + c : at_decay + c + 1, :rows]

    def update(first):
        for at in range(0, batch, 128):
            write = write_ref[:, at : at + 128]
            decay = decay_ref[:, at : at + 128]
            for k in range(slab):
                row = key_ref[key_rows + first + k : key_rows + first + k + 1, at : at + 128]
                out_ref[k, :, at : at + 128] = decay * state_ref[k, :, at : at + 128] + row * write

    for part in range(key_rows // slab):
        pl.when(step == part)(functools.partial(update, part * slab))


def state_update(landed, sent, state):
    key_rows, half, batch = state.shape
    slab = 4
    block = pl.BlockSpec((slab, half, batch), lambda i: (i, 0, 0))
    return pl.pallas_call(
        state_update_kernel,
        grid=(key_rows // slab,),
        in_specs=[
            pl.BlockSpec(landed.shape, lambda i: (0, 0, 0)),
            pl.BlockSpec(sent.shape, lambda i: (0, 0, 0)),
            block,
        ],
        out_specs=block,
        out_shape=jax.ShapeDtypeStruct(state.shape, jnp.float32),
        scratch_shapes=[
            pltpu.VMEM((2 * key_rows, batch), jnp.float32),
            pltpu.VMEM((half, batch), jnp.float32),
            pltpu.VMEM((1, batch), jnp.float32),
        ],
        compiler_params=pltpu.CompilerParams(vmem_limit_bytes=12 * 1024 * 1024),
        cost_estimate=pl.CostEstimate(
            flops=3 * state.size, bytes_accessed=8 * state.size, transcendentals=0
        ),
    )(landed, sent, pltpu.with_memory_space_constraint(state, pltpu.HBM))


def per_device(
    hidden_in,
    state,
    attn_norm_gain,
    w_query,
    w_key,
    w_value,
    w_gate,
    w_decay,
    w_beta,
    decay_log,
    decay_bias,
    head_gain,
    w_out,
    final_gain,
    lm_weight,
    token_ids,
    ref_logprob,
):
    core = lax.axis_index(CORE)
    zed = lax.axis_index(Z)
    head = lax.axis_index(XY)
    n_xy = lax.axis_size(XY)
    n_z = lax.axis_size(Z)
    key_rows, half, batch = state.shape
    rows = hidden_in.shape[0] // 2
    vocab_dev = lm_weight.shape[1]

    x_chip = in_core_order(core, hidden_in, swapped(hidden_in), 1)
    gain_chip = in_core_order(core, final_gain, swapped(final_gain), 0)
    x_block = lax.dynamic_slice_in_dim(x_chip, core * rows, rows, 0)
    x_block = jnp.concatenate([x_block, gain_chip[None, :]])

    out_full = lax.all_gather(w_out, ROW, axis=0, tiled=True)
    weights = (w_query, w_key, w_value, w_gate)
    copies = jnp.broadcast_to(x_block, (lax.axis_size(XY), *x_block.shape))
    copies, weights, attn_norm_gain = lax.optimization_barrier((copies, weights, attn_norm_gain))
    pieces = exchange(copies, XY)
    w_other, weights = lax.optimization_barrier(([swapped(w) for w in weights], weights))
    w_own = jnp.concatenate(weights, axis=1)
    w_other = jnp.concatenate(w_other, axis=1)

    x_full = jnp.moveaxis(pieces[:, :rows], 0, 1).reshape(rows, D).astype(jnp.float32)
    normed = (
        x_full
        * lax.rsqrt(jnp.mean(x_full * x_full, axis=1, keepdims=True) + 1e-06)
        * attn_norm_gain.astype(jnp.float32)
    ).astype(jnp.bfloat16)

    def project(weight):
        return lax.dot_general(
            weight, normed, (((0,), (1,)), ((), ())), preferred_element_type=jnp.float32
        )

    own = project(w_own).reshape(4, half, rows)
    other = project(w_other).reshape(4, half, rows)
    qkvg = in_core_order(core, own, other, 1)
    raw = lax.optimization_barrier(qkvg[:2].astype(jnp.bfloat16)).astype(jnp.float32)
    unit = (raw * lax.rsqrt(jnp.sum(raw * raw, axis=1, keepdims=True) + 1e-06)).astype(
        jnp.bfloat16
    )

    unit_pair = in_core_order(core, unit, swapped(unit), 2)
    parts = jnp.moveaxis(unit_pair.reshape(2, n_z, key_rows, 2 * rows), 1, 0)
    parts = parts.reshape(n_z, 2 * key_rows, 2 * rows)
    parts, lm_weight, after = lax.optimization_barrier((parts, lm_weight, head_gain))
    state_held = held([state], after)
    lm_other = swapped(lm_weight)
    landed = exchange(parts, Z)

    both = state_sums(landed, state_held)
    small_in = (w_decay, w_beta, decay_log, decay_bias, token_ids, pieces, head_gain)
    both, lm_weight, lm_other, small_in = lax.optimization_barrier(
        (both, lm_weight, lm_other, small_in)
    )
    w_decay, w_beta, decay_log, decay_bias, token_ids, pieces, head_gain = small_in
    lm_both = held([lm_weight, lm_other], head_gain)
    gain_full = pieces[:, rows].reshape(D).astype(jnp.float32)
    both = exchange(both.reshape(n_z, 2 * rows, 2 * half), Z)
    both = jnp.sum(both.astype(jnp.float32), axis=0)

    small = project(jnp.concatenate([w_decay, w_beta], axis=1))
    alpha = jnp.exp(
        -jnp.exp(decay_log)[:, None] * jax.nn.softplus(small[:HEADS] + decay_bias[:, None])
    )
    alpha = lax.dynamic_slice_in_dim(alpha, head, 1, 0)
    beta = lax.dynamic_slice_in_dim(jax.nn.sigmoid(small[HEADS:]), head, 1, 0)
    unit_f = unit.astype(jnp.float32)
    meet = jnp.sum(unit_f[0] * unit_f[1], axis=0, keepdims=True)
    value, gate = qkvg[2].T, qkvg[3].T
    columns = jnp.concatenate([alpha, beta, meet]).T
    alpha_c, beta_c, meet_c = columns[:, :1], columns[:, 1:2], columns[:, 2:]

    kept = lax.dynamic_slice_in_dim(both, core * rows, rows, 0)
    given = lax.dynamic_slice_in_dim(both, (1 - core) * rows, rows, 0)
    given = swapped(given)
    recall = in_core_order(core, kept[:, :half], given[:, :half], 1)
    answer = in_core_order(core, kept[:, half:], given[:, half:], 1)
    write = beta_c * (value - alpha_c * recall)
    readout = alpha_c * answer + meet_c * write
    power = jnp.mean(readout * readout, axis=1, keepdims=True)
    mixed = (
        readout * lax.rsqrt(power + 1e-05) * head_gain[None, :] * jax.nn.silu(gate)
    ).astype(jnp.bfloat16)

    mixed_full = jnp.moveaxis(to_all(mixed, XY), 0, 1).reshape(rows, D)
    hidden = x_full + jnp.dot(mixed_full, out_full, preferred_element_type=jnp.float32)
    energy = jnp.mean(hidden * hidden, axis=1, keepdims=True)
    final = (hidden * lax.rsqrt(energy + 1e-06) * gain_full[None, :]).astype(jnp.bfloat16)

    ids = lax.dynamic_index_in_dim(token_ids.reshape(n_z, 2, rows), core, 1, False)
    ids = lax.dynamic_slice_in_dim(jnp.concatenate([ids, ids]), zed, n_z, 0).T

    own_start = ((head * 2 + core) * n_z + zed) * vocab_dev
    other_start = ((head * 2 + 1 - core) * n_z + zed) * vocab_dev

    def statistics(block, ids):
        logits = jnp.dot(block, lm_both, preferred_element_type=jnp.float32)
        at = lax.broadcasted_iota(jnp.int32, logits.shape, 1)
        at = at + jnp.where(at < vocab_dev, own_start, other_start - vocab_dev)
        picked = jnp.sum(jnp.where(at == ids, logits, jnp.zeros_like(logits)), axis=1)
        top = jnp.max(logits, axis=1)
        expo = jnp.exp(logits - top[:, None])
        return jnp.stack([top, jnp.sum(expo, axis=1), jnp.sum(expo * logits, axis=1), picked])

    def along_z(block, step):
        return lax.ppermute(block, Z, [(k, (k + step) % n_z) for k in range(n_z)])

    middle = n_z // 2
    by_distance = [None] * n_z
    up = down = (final[:, : D // 2], final[:, D // 2 :])
    for step in range(1, middle):
        pairs = [(along_z(u, 1), along_z(d, -1)) for u, d in zip(up, down)]
        up, down = zip(*pairs)
        block = jnp.concatenate([jnp.concatenate(p) for p in pairs], axis=1)
        back = n_z - step
        two = statistics(
            block, jnp.concatenate([ids[:, back : back + 1], ids[:, step : step + 1]])
        )
        by_distance[back], by_distance[step] = two[:, :rows], two[:, rows:]
    block = jnp.concatenate([along_z(up[0], 1), along_z(down[1], -1)], axis=1)
    two = statistics(
        jnp.concatenate([final, block]), jnp.concatenate([ids[:, :1], ids[:, middle : middle + 1]])
    )
    by_distance[0], by_distance[middle] = two[:, :rows], two[:, rows:]
    stats = jnp.stack(by_distance)
    stats = lax.dynamic_slice_in_dim(jnp.concatenate([stats, stats]), n_z - zed, n_z, 0)
    stats = jnp.moveaxis(stats, 1, 0).reshape(4, n_z * rows)

    kept = lax.dynamic_slice_in_dim(write, core * half, half, 1)
    given = lax.dynamic_slice_in_dim(write, (1 - core) * half, half, 1)
    w_block = in_core_order(core, kept, swapped(given), 1)
    a_block = in_core_order(core, alpha, swapped(alpha), 0)
    lanes = 2 * half
    n_stats = 4 * n_z * rows // lanes
    a_block = jnp.pad(a_block, ((0, 0), (0, lanes - rows)))
    tail = jnp.concatenate([stats.reshape(n_stats, lanes), a_block])
    tail = jnp.pad(tail, ((0, -tail.shape[0] % 8), (0, 0)))
    sent = to_all(jnp.concatenate([w_block, tail]), Z)
    stats = sent[:, rows : rows + n_stats].reshape(n_z, 4, n_z * rows)
    stats = jnp.stack(merged(jnp.moveaxis(stats, 1, 0), 0))
    copies = jnp.broadcast_to(stats, (lax.axis_size(XY), *stats.shape))
    copies, sent = lax.optimization_barrier((copies, sent))
    shared = exchange(copies, XY)

    new_state = state_update(landed, sent, state)
    shared, new_state = lax.optimization_barrier((shared, new_state))
    top, total, weighted, picked = merged(jnp.moveaxis(shared, 1, 0), 0)
    lse = top + jnp.log(total)
    mine = jnp.stack([picked - lse, lse - weighted / total])
    logprob, entropy = in_core_order(core, mine[:, None], swapped(mine)[:, None], 1)

    def in_order(two):
        return jnp.moveaxis(two.reshape(2, n_z, rows), 0, 1).reshape(batch)

    logprob = in_order(logprob)
    entropy = in_order(entropy)
    gap = jnp.clip(ref_logprob - logprob, -20.0, 20.0)
    kl = jnp.minimum(jnp.exp(gap) - gap - 1.0, 10.0)
    return (new_state, logprob, entropy, kl)


def solution(mesh):
    split = Mesh(mesh.devices.reshape(4, 4, 2, mesh.shape["col"]), (X, Y, CORE, Z))
    in_specs = (
        P(Z, ROW),
        P(Z, ROW, None),
        P(),
        P(None, ROW),
        P(None, ROW),
        P(None, ROW),
        P(None, ROW),
        P(),
        P(),
        P(),
        P(),
        P(),
        P(ROW, None),
        P(ROW),
        P(None, ROW_COL),
        P(),
        P(),
    )
    out_specs = (P(Z, ROW, None), P(), P(), P())
    return jax.shard_map(
        per_device, mesh=split, in_specs=in_specs, out_specs=out_specs, check_vma=False
    )
```
